32 devices in a mesh: dp: 16 (over z, x, core), tensor: 2 (over y).
Axes of the slice: x: 2, y: 2, z: 4, core: 2. Of those that a mesh axis runs over, the one named last changes fastest.
Arguments:
- residual_in: float32 [16384, 1536], P(('dp', 'tensor')), may hold values from -6 to 6
- cotangent: float32 [16384, 1536], P(('dp', 'tensor')), may hold values from -6 to 6
- input_gain: float32 [2, 1536], replicated, may hold values from 0.5 to 1.5
- z_weight: bfloat16 [2, 1536, 3072], P(None, 'dp', 'tensor'), may hold values from -0.15625 to 0.15625
- x_weight: bfloat16 [2, 1536, 3072], P(None, 'dp', 'tensor'), may hold values from -0.15625 to 0.15625
- bc_weight: bfloat16 [2, 1536, 256], P(None, ('dp', 'tensor')), may hold values from -0.15625 to 0.15625
- dt_weight: bfloat16 [2, 1536, 48], P(None, 'dp', 'tensor'), may hold values from -0.15625 to 0.15625
- conv_inner: float32 [2, 4, 3072], P(None, None, 'tensor'), may hold values from -3 to 3
- conv_inner_bias: float32 [2, 3072], P(None, 'tensor'), may hold values from -1.5 to 1.5
- conv_state: float32 [2, 4, 256], replicated, may hold values from -3 to 3
- conv_state_bias: float32 [2, 256], replicated, may hold values from -1.5 to 1.5
- dt_bias: float32 [2, 48], P(None, 'tensor'), may hold values from -8.2 to -2.2
- decay_log: float32 [2, 48], P(None, 'tensor'), may hold values from 0 to 2.77
- skip_gain: float32 [2, 48], P(None, 'tensor'), may hold values from 0.1 to 1.9
- gated_gain: float32 [2, 3072], P(None, 'tensor'), may hold values from 0.5 to 1.5
- out_weight: bfloat16 [2, 3072, 1536], P(None, 'tensor', 'dp'), may hold values from -0.109375 to 0.109375
Outputs:
- output: float32 [16384, 1536], P(('dp', 'tensor'))
- grad_in: float32 [16384, 1536], P(('dp', 'tensor'))
- grad_input_gain: float32 [2, 1536], replicated
- grad_z_weight: float32 [2, 1536, 3072], P(None, 'dp', 'tensor')
- grad_x_weight: float32 [2, 1536, 3072], P(None, 'dp', 'tensor')
- grad_bc_weight: float32 [2, 1536, 256], P(None, ('dp', 'tensor'))
- grad_dt_weight: float32 [2, 1536, 48], P(None, 'dp', 'tensor')
- grad_conv_inner: float32 [2, 4, 3072], P(None, None, 'tensor')
- grad_conv_inner_bias: float32 [2, 3072], P(None, 'tensor')
- grad_conv_state: float32 [2, 4, 256], replicated
- grad_conv_state_bias: float32 [2, 256], replicated
- grad_dt_bias: float32 [2, 48], P(None, 'tensor')
- grad_decay_log: float32 [2, 48], P(None, 'tensor')
- grad_skip_gain: float32 [2, 48], P(None, 'tensor')
- grad_gated_gain: float32 [2, 3072], P(None, 'tensor')
- grad_out_weight: float32 [2, 3072, 1536], P(None, 'tensor', 'dp')
The draws below stay inside these ranges and needn't reach their ends.
All inputs are finite; a program needn't handle non-finite values.
Results may differ from the reference program's by a relative error of at most 0.014.
Values may be sent and summed in bfloat16 or wider, within the bound.
No kernel may reach another device: no remote copies, remote signals or barrier semaphores. Data moves between devices by JAX's collectives and lax.ppermute only.
A program may use at most 320 MiB of HBM per device.

```python
import math
import jax
import jax.numpy as jnp
from jax import lax

D = 1536
HEADS = 48
HEADDIM = 64
STATE = 128
CONV = 4
SPAN = 256
LAYERS = 2
SEQ = 1024
INNER = 3072
TOKENS = 16384


def draw_dt_bias(key, part):
    key = jax.random.fold_in(key, 7)
    lower_end = math.log(0.001)
    upper_end = math.log(0.1)
    exponent = jax.random.uniform(key, (LAYERS, HEADS), jnp.float32, lower_end, upper_end)
    return jnp.log(jnp.expm1(jnp.exp(exponent)))


def spiked(array, key, source, target, parts, factor):
    def block_of(position):
        return (jnp.arange(array.shape[position]) // (array.shape[position] // parts)).reshape((-1,) + (1,) * (array.ndim - 1 - position))

    first = jax.random.permutation(key, parts)[block_of(target)]
    far = (block_of(target) + parts // 2) % parts
    return jnp.where((block_of(source) == first) | (block_of(source) == far), factor * array, array)


def level_of(own_key, shape, split, smallest, top_value):
    level = 1.0
    for axis_at, parts in split:
        heights = jax.random.uniform(jax.random.fold_in(jax.random.fold_in(own_key, 6), axis_at), (parts,), jnp.float32, smallest / len(split), top_value / len(split))
        level = level * jnp.repeat(jnp.exp(heights), shape[axis_at] // parts).reshape((-1,) + (1,) * (len(shape) - 1 - axis_at))
    return level


def scatter_about(own_key, shape, scale, bound, split=(), dtype=jnp.bfloat16):
    loudness = level_of(own_key, shape, split, -0.22, 0.18) if split else 1.0
    entries = jax.random.normal(own_key, shape, jnp.float32) * scale * loudness
    return jnp.minimum(jnp.maximum(entries, -bound), bound).astype(dtype)


def bell_draw_with(rng, dims, spread, bound, shards, heavy, dtype=jnp.bfloat16):
    drawn = spread * jax.random.normal(rng, dims, jnp.float32)
    if shards:
        drawn = drawn * level_of(rng, dims, shards, -0.22, 0.18)
    return jnp.clip(spiked(drawn, jax.random.fold_in(rng, 3), *heavy), -bound, bound).astype(dtype)


def setup_inputs(seed: int = 0) -> dict:
    seeds = jax.random.split(jax.random.key(seed), 17)
    return {
        "residual_in": bell_draw_with(seeds[0], (TOKENS, D), 1.0, 6.0, ((0, 32),), (0, 1, 32, 2.75), jnp.float32),
        "cotangent": scatter_about(seeds[1], (TOKENS, D), 1.0, 6.0, ((0, 32),), jnp.float32),
        "input_gain": jnp.clip(1.0 + 0.1 * jax.random.normal(seeds[2], (LAYERS, D), jnp.float32), 0.5, 1.5),
        "z_weight": scatter_about(seeds[3], (LAYERS, D, INNER), D ** -0.5, 0.15625, ((1, 16), (2, 2))),
        "x_weight": scatter_about(seeds[4], (LAYERS, D, INNER), D ** -0.5, 0.15625, ((1, 16), (2, 2))),
        "bc_weight": scatter_about(seeds[5], (LAYERS, D, 2 * STATE), D ** -0.5, 0.15625, ((1, 32),)),
        "dt_weight": scatter_about(seeds[6], (LAYERS, D, HEADS), D ** -0.5, 0.15625, ((1, 16), (2, 2))),
        "conv_inner": scatter_about(seeds[7], (LAYERS, CONV, INNER), CONV ** -0.5, 3.0, ((2, 2),), jnp.float32),
        "conv_inner_bias": scatter_about(seeds[8], (LAYERS, INNER), 0.3, 1.5, ((1, 2),), jnp.float32),
        "conv_state": scatter_about(seeds[9], (LAYERS, CONV, 2 * STATE), CONV ** -0.5, 3.0, (), jnp.float32),
        "conv_state_bias": scatter_about(seeds[10], (LAYERS, 2 * STATE), 0.3, 1.5, (), jnp.float32),
        "dt_bias": draw_dt_bias(jax.random.fold_in(seeds[16], 71), 0),
        "decay_log": jnp.clip(2.77 * jax.random.uniform(seeds[12], (LAYERS, HEADS), jnp.float32) ** level_of(seeds[12], (LAYERS, HEADS), ((1, 2),), -0.2, 0.2), 0.0, 2.77),
        "skip_gain": jnp.clip(1.0 + 0.18 * jax.random.normal(seeds[13], (LAYERS, HEADS), jnp.float32), 0.1, 1.9),
        "gated_gain": jnp.clip(1.0 + 0.1 * jax.random.normal(seeds[14], (LAYERS, INNER), jnp.float32), 0.5, 1.5),
        "out_weight": scatter_about(seeds[15], (LAYERS, INNER, D), INNER ** -0.5, 0.109375, ((1, 2), (2, 16))),
    }


@jax.custom_vjp
def low(v):
    return lax.optimization_barrier(v.astype(jnp.bfloat16)).astype(jnp.float32)

@jax.custom_vjp
def low_back(v):
    return v

def low_keep(v):
    return (low(v), None)

def low_pass(kept, grad):
    return (grad,)

def back_keep(v):
    return (v, None)

def back_low(kept, grad):
    return (low(grad),)
low.defvjp(low_keep, low_pass)
low_back.defvjp(back_keep, back_low)
epsilon = 1e-05
highest = lax.Precision.HIGHEST

def matmul(left_side, right_side):
    return jnp.dot(left_side, right_side, precision=highest, preferred_element_type=jnp.float32)

def causal_conv(values, kernel, offset):
    taps = kernel.shape[0]
    length = values.shape[0]
    padded = jnp.pad(values, ((taps - 1, 0), (0, 0)))
    running = jnp.zeros_like(values) + offset
    for index in range(taps):
        running = running + kernel[index] * padded[index:index + length]
    return running

def state_space(inner_act, step_size, decay_rate, key_rows, query_rows, block_len, head_size):
    length, channels = inner_act.shape
    head_count = step_size.shape[1]
    blocks = length // block_len
    values = inner_act.reshape(blocks, block_len, head_count, head_size)
    log_rates = (step_size * decay_rate).reshape(blocks, block_len, head_count)
    step_blocks = step_size.reshape(blocks, block_len, head_count)
    key_blocks = key_rows.reshape(blocks, block_len, -1)
    query_blocks = query_rows.reshape(blocks, block_len, -1)
    cumulative = jnp.cumsum(log_rates, axis=1)
    log_gaps = cumulative[:, :, None, :] - cumulative[:, None, :, :]
    causal_mask = jnp.tril(jnp.ones((block_len, block_len), jnp.bool_))[None, :, :, None]
    decay_mask = jnp.exp(jnp.where(causal_mask, log_gaps, -1e+30))
    affinity = jnp.einsum('cis,cjs->cij', query_blocks, key_blocks, precision=highest)
    mixing = affinity[..., None] * decay_mask * step_blocks[:, None, :, :]
    within = jnp.einsum('cijh,cjhp->cihp', mixing, values, precision=highest)
    tail_weights = jnp.exp(cumulative[:, -1:, :] - cumulative) * step_blocks
    weighted_values = values * tail_weights[..., None]
    block_states = jnp.einsum('cjs,cjhp->chps', key_blocks, weighted_values, precision=highest)
    block_decay = jnp.exp(cumulative[:, -1, :])

    def carry_step(carried, inputs):
        factor, fresh_state = inputs
        return (factor[:, None, None] * carried + fresh_state, carried)
    initial = jnp.zeros((head_count, head_size, key_rows.shape[1]), jnp.float32)
    final_state, before = lax.scan(carry_step, initial, (block_decay, block_states))
    across = jnp.einsum('cis,chps->cihp', query_blocks, before, precision=highest) * jnp.exp(cumulative)[..., None]
    return (within + across).reshape(length, channels)

def layer_forward(residual, layer_params):
    input_gain, z_weight, x_weight, bc_weight, dt_weight, conv_inner, conv_inner_bias, conv_state, conv_state_bias, dt_bias, decay_log, skip_gain, gated_gain, out_weight = layer_params
    norm_scale = lax.rsqrt(lax.optimization_barrier(jnp.mean(residual * residual, axis=-1, keepdims=True)) + epsilon)
    normed = low(residual * norm_scale * input_gain)
    gate_proj = low_back(matmul(normed, z_weight))
    inner_raw = low_back(matmul(normed, x_weight))
    state_raw = low_back(matmul(normed, bc_weight))
    step_raw = low_back(matmul(normed, dt_weight))
    inner_act = low(jax.nn.silu(causal_conv(inner_raw, conv_inner, conv_inner_bias)))
    state_act = low(jax.nn.silu(causal_conv(state_raw, conv_state, conv_state_bias)))
    half_width = state_act.shape[1] // 2
    step_size = jax.nn.softplus(step_raw + dt_bias)
    decay_rate = -jnp.exp(decay_log)
    mixed_out = state_space(inner_act, step_size, decay_rate, state_act[:, :half_width], state_act[:, half_width:], SPAN, HEADDIM)
    mixed_out = mixed_out + inner_act * jnp.repeat(skip_gain, HEADDIM)
    gated = mixed_out * jax.nn.silu(gate_proj)
    factor = lax.rsqrt(lax.optimization_barrier(jnp.mean(gated * gated, axis=-1, keepdims=True)) + epsilon)
    normed_out = low(gated * factor * gated_gain)
    return residual + low_back(matmul(normed_out, out_weight))

def reference(residual_in, cotangent, input_gain, z_weight, x_weight, bc_weight, dt_weight, conv_inner, conv_inner_bias, conv_state, conv_state_bias, dt_bias, decay_log, skip_gain, gated_gain, out_weight):
    weights = (input_gain.astype(jnp.float32), z_weight.astype(jnp.float32), x_weight.astype(jnp.float32), bc_weight.astype(jnp.float32), dt_weight.astype(jnp.float32), conv_inner.astype(jnp.float32), conv_inner_bias.astype(jnp.float32), conv_state.astype(jnp.float32), conv_state_bias.astype(jnp.float32), dt_bias.astype(jnp.float32), decay_log.astype(jnp.float32), skip_gain.astype(jnp.float32), gated_gain.astype(jnp.float32), out_weight.astype(jnp.float32))

    def forward(inputs, layer_weights):
        sequences = inputs.reshape(inputs.shape[0] // SEQ, SEQ, inputs.shape[1])

        def one_sequence(rows_in):
            current = rows_in
            for layer_idx in range(LAYERS):
                current = layer_forward(current, tuple((member[layer_idx] for member in layer_weights)))
            return current
        return lax.map(jax.checkpoint(one_sequence), sequences).reshape(inputs.shape)
    output, pullback = jax.vjp(forward, residual_in.astype(jnp.float32), weights)
    grad_in, grads = pullback(cotangent.astype(jnp.float32))
    return (output, grad_in, grads[0], grads[1], grads[2], grads[3], grads[4], grads[5], grads[6], grads[7], grads[8], grads[9], grads[10], grads[11], grads[12], grads[13])
```

```python
import jax
import jax.numpy as jnp
from jax import lax
from jax.experimental import pallas as pl
from jax.experimental.pallas import tpu as pltpu
from jax.sharding import PartitionSpec as P

HEADDIM = 64
CHUNK = 128
LANES = 128
epsilon = 1e-05
highest = lax.Precision.HIGHEST
f32 = jnp.float32
bf16 = jnp.bfloat16


def dot_nn(left, right):
    return lax.dot_general(left, right, (((1,), (0,)), ((), ())), preferred_element_type=f32)


def dot_nt(left, right):
    return lax.dot_general(left, right, (((1,), (1,)), ((), ())), preferred_element_type=f32)


def dot_tn(left, right):
    return lax.dot_general(left, right, (((0,), (0,)), ((), ())), preferred_element_type=f32)


def conv_rows(ext, kernel, offset, length):
    total = offset + kernel[0:1] * ext[5 : 5 + length]
    for tap in range(1, 4):
        total = total + kernel[tap : tap + 1] * ext[5 + tap : 5 + tap + length]
    return total


def row_col(size):
    return (
        lax.broadcasted_iota(jnp.int32, (size, size), 0),
        lax.broadcasted_iota(jnp.int32, (size, size), 1),
    )


def decays(dt_ref, rate_ref, lower):
    step = dt_ref[...]
    cum = lax.dot_general(
        lower, step * rate_ref[...], (((1,), (0,)), ((), ())), precision=highest,
        preferred_element_type=f32,
    )
    last = cum[CHUNK - 1 : CHUNK]
    return step, cum, cum.T, last, jnp.exp(cum), jnp.exp(last - cum)


def forward_kernel(
    rot_ref, xr_ref, bcr_ref, dt_ref, zr_ref,
    cw_ref, cb_ref, sw_ref, sb_ref, rate_ref, skip_ref, gain_ref,
    ghat_ref, ssq_ref, y_ref, s_ref,
    state, x_halo, bc_halo,
):
    @pl.when(pl.program_id(0) == 0)
    def _():
        state[...] = jnp.zeros_like(state)
        x_halo[...] = jnp.zeros_like(x_halo)
        bc_halo[...] = jnp.zeros_like(bc_halo)

    rows, cols = row_col(CHUNK)
    causal = rows >= cols
    low_half = cols < HEADDIM
    step, cum, cum_t, last, grow, tail = decays(dt_ref, rate_ref, jnp.where(causal, 1.0, 0.0))
    tail_step = tail * step
    last_grow = jnp.exp(last)
    bc_ext = jnp.concatenate([bc_halo[...], bcr_ref[...]], axis=0)
    bc_halo[...] = bcr_ref[CHUNK - 8 :]
    bc_pre = conv_rows(bc_ext, sw_ref[...], sb_ref[...], CHUNK)
    bc = (bc_pre * jax.nn.sigmoid(bc_pre)).astype(bf16)
    b_low, c_low = bc[:, :LANES], bc[:, LANES:]
    c_wide = c_low.astype(f32)
    b_turned = b_low.astype(f32).T.astype(bf16)
    mix = jnp.where(causal, dot_nt(c_low, b_low), 0.0)
    squares = jnp.zeros((CHUNK, LANES), f32)

    def spread(cols_of, head):
        return jnp.where(low_half, cols_of[:, head : head + 1], cols_of[:, head + 1 : head + 2])

    for pair in range(xr_ref.shape[1] // LANES):
        at = slice(pair * LANES, (pair + 1) * LANES)
        head = 2 * pair
        xr = xr_ref[:, at]
        ext = jnp.concatenate([x_halo[:, at], xr], axis=0)
        x_halo[:, at] = xr[CHUNK - 8 :]
        pre = conv_rows(ext, cw_ref[:, at], cb_ref[:, at], CHUNK)
        x = (pre * jax.nn.sigmoid(pre)).astype(bf16).astype(f32)
        x_step = (x * spread(step, head)).astype(bf16)
        s_in = state[:, at]
        s_low = s_in.astype(bf16)
        s_ref[0, :, at] = s_low
        right = jnp.concatenate([x_step, s_low], axis=0)
        parts = []
        for h in (head, head + 1):
            decay = jnp.exp(jnp.minimum(cum[:, h : h + 1] - cum_t[h : h + 1, :], 0.0))
            left = jnp.concatenate(
                [(mix * decay).astype(bf16), (c_wide * grow[:, h : h + 1]).astype(bf16)], axis=1
            )
            parts.append(dot_nn(left, right))
        y = jnp.where(low_half, parts[0], parts[1]) + skip_ref[:, at] * x
        y_ref[:, at] = y
        z = zr_ref[:, at]
        gated = y * (z * jax.nn.sigmoid(z))
        squares = squares + gated * gated
        ghat_ref[:, at] = (gated * gain_ref[:, at]).astype(bf16)
        fresh = dot_nn(b_turned, (x * spread(tail_step, head)).astype(bf16))
        state[:, at] = s_in * spread(last_grow, head)[0:1] + fresh
    ssq_ref[0] = jnp.sum(squares.T, axis=0, keepdims=True)


def backward_kernel(
    rot_ref, xr_ref, xp_ref, bcr_ref, bcp_ref, dt_ref, sig_ref, zr_ref, y_ref, s_ref, dyn_ref, q_ref, qc_ref,
    cw_ref, cb_ref, sw_ref, sb_ref, rate_ref, skip_ref, gain_ref,
    dz_ref, dp_ref, gx_ref, gs_ref, gh_ref,
    dstate, s_next, x_halo, bc_halo, tally,
):
    inner = xr_ref.shape[1]
    first = pl.program_id(0) == pl.num_programs(0) - 1

    @pl.when(pl.program_id(0) == 0)
    def _():
        dstate[...] = jnp.zeros_like(dstate)
        s_next[...] = jnp.zeros_like(s_next)
        x_halo[...] = jnp.zeros_like(x_halo)
        bc_halo[...] = jnp.zeros_like(bc_halo)
        gx_ref[...] = jnp.zeros_like(gx_ref)
        gs_ref[...] = jnp.zeros_like(gs_ref)
        gh_ref[...] = jnp.zeros_like(gh_ref)

    rows, cols = row_col(CHUNK)
    upper = cols >= rows
    low_half = cols < HEADDIM
    keep = jnp.where(first, 0.0, 1.0)
    step, cum, cum_t, last, grow, tail = decays(dt_ref, rate_ref, jnp.where(rows >= cols, 1.0, 0.0))
    tail_step = tail * step
    last_grow = jnp.exp(last)
    bcr = bcr_ref[...]
    bc_ext = jnp.concatenate([bcp_ref[...] * keep, bcr], axis=0)
    bc_pre = conv_rows(bc_ext, sw_ref[...], sb_ref[...], CHUNK)
    bc_sig = jax.nn.sigmoid(bc_pre)
    bc = (bc_pre * bc_sig).astype(bf16)
    b_low, c_low = bc[:, :LANES], bc[:, LANES:]
    b_wide = b_low.astype(f32)
    c_turned = c_low.astype(f32).T.astype(bf16)
    mix = jnp.where(upper, dot_nt(b_low, c_low), 0.0)
    q = jnp.broadcast_to(q_ref[0], (CHUNK, CHUNK)).T
    qc = jnp.broadcast_to(qc_ref[0], (CHUNK, CHUNK)).T

    def spread(cols_of, head):
        return jnp.where(low_half, cols_of[:, head : head + 1], cols_of[:, head + 1 : head + 2])

    def two_parts(values):
        high = values.astype(bf16)
        return jnp.concatenate([high, (values - high.astype(f32)).astype(bf16)], axis=1)

    def add_to(ref, index, at, values):
        ref[index : index + 1, at] += jnp.sum(values, axis=0, keepdims=True)

    d_mix = jnp.zeros((CHUNK, CHUNK), f32)
    d_b = jnp.zeros((CHUNK, LANES), f32)
    d_c = jnp.zeros((CHUNK, LANES), f32)
    d_cum = jnp.zeros((CHUNK, LANES), f32)
    d_direct = jnp.zeros((CHUNK, LANES), f32)
    through = jnp.zeros((8, LANES), f32)
    sel_rows = lax.broadcasted_iota(jnp.int32, (2 * LANES, LANES), 0)
    sel_cols = lax.broadcasted_iota(jnp.int32, (2 * LANES, LANES), 1)
    sel_head = jnp.where(sel_rows % LANES < HEADDIM, 0, 1)
    for pair in range(inner // LANES):
        at = slice(pair * LANES, (pair + 1) * LANES)
        head = 2 * pair
        select = jnp.where(sel_cols == sel_head + head, 1.0, 0.0).astype(bf16)
        xr = xr_ref[:, at]
        ext = jnp.concatenate([xp_ref[:, at] * keep, xr], axis=0)
        pre = conv_rows(ext, cw_ref[:, at], cb_ref[:, at], CHUNK)
        sig = jax.nn.sigmoid(pre)
        x_low = (pre * sig).astype(bf16)
        x = x_low.astype(f32)
        step_wide = spread(step, head)
        x_step = (x * step_wide).astype(bf16)
        z = zr_ref[:, at]
        z_sig = jax.nn.sigmoid(z)
        z_act = z * z_sig
        y = y_ref[:, at]
        gated = y * z_act
        dyn = dyn_ref[:, at]
        add_to(gx_ref, 6, at, dyn * gated * q)
        d_gated = dyn * (gain_ref[:, at] * q) - gated * qc
        dz_ref[:, at] = (d_gated * y * (z_sig * (1.0 + z * (1.0 - z_sig)))).astype(bf16)
        dy = d_gated * z_act
        dy_low = dy.astype(bf16)
        dy_wide = dy_low.astype(f32)
        add_to(gx_ref, 5, at, dy * x)
        ds = dstate[:, at]
        ds_low = ds.astype(bf16)
        right = jnp.concatenate([dy_low, ds_low], axis=0)
        parts = []
        zero = jnp.zeros_like(x_step)
        for h in (head, head + 1):
            decay = jnp.exp(jnp.minimum(cum_t[h : h + 1, :] - cum[:, h : h + 1], 0.0))
            left = jnp.concatenate(
                [(mix * decay).astype(bf16), (b_wide * tail[:, h : h + 1]).astype(bf16)], axis=1
            )
            parts.append(dot_nn(left, right))
            own = jnp.where(low_half, x_step, zero) if h == head else jnp.where(low_half, zero, x_step)
            d_mix = d_mix + dot_nt(own, dy_low) * decay
        u = jnp.where(low_half, parts[0], parts[1])
        skip = skip_ref[:, at]
        dx = step_wide * u + skip * dy
        d_cum = d_cum + dot_nn(
            two_parts(dy_wide * (y - skip * x) - x_step.astype(f32) * u), select
        )
        d_direct = d_direct + dot_nn(two_parts(x * u), select)
        s_out = s_next[:, at].astype(f32)
        s_low = s_ref[0, :, at]
        s_next[:, at] = s_low
        crossing = jnp.sum(ds * s_out, axis=0, keepdims=True)
        through = through + dot_nn(two_parts(jnp.broadcast_to(crossing, (8, LANES))), select)
        dy_grow = (dy_wide * spread(grow, head)).astype(bf16)
        d_c = d_c + dot_nt(dy_grow, s_low)
        d_b = d_b + dot_nt((x * spread(tail_step, head)).astype(bf16), ds_low)
        dstate[:, at] = ds * spread(last_grow, head)[0:1] + dot_nn(c_turned, dy_grow)
        d_pre = dx * (sig * (1.0 + pre * (1.0 - sig)))
        d_ext = jnp.concatenate([d_pre, x_halo[:, at]], axis=0)
        x_halo[:, at] = d_pre[:8]
        d_raw = cw_ref[3:4, at] * d_pre
        for tap in range(3):
            d_raw = d_raw + cw_ref[tap : tap + 1, at] * d_ext[3 - tap : 3 - tap + CHUNK]
            add_to(gx_ref, tap, at, d_pre * ext[5 + tap : 5 + tap + CHUNK])
        add_to(gx_ref, 3, at, d_pre * xr)
        add_to(gx_ref, 4, at, d_pre)
        dp_ref[:, at] = d_raw.astype(bf16)
    d_mix = jnp.where(upper, d_mix, 0.0)
    d_b = d_b + dot_nn(d_mix.astype(bf16), c_low)
    d_c = d_c + dot_nn(d_mix.T.astype(bf16), b_low)
    d_bc = jnp.concatenate([d_b, d_c], axis=1)
    d_pre = d_bc * (bc_sig * (1.0 + bc_pre * (1.0 - bc_sig)))
    d_ext = jnp.concatenate([d_pre, bc_halo[...]], axis=0)
    bc_halo[...] = d_pre[:8]
    d_raw = sw_ref[3:4] * d_pre
    whole = slice(None)
    for tap in range(3):
        d_raw = d_raw + sw_ref[tap : tap + 1] * d_ext[3 - tap : 3 - tap + CHUNK]
        add_to(gs_ref, tap, whole, d_pre * bc_ext[5 + tap : 5 + tap + CHUNK])
    add_to(gs_ref, 3, whole, d_pre * bcr)
    add_to(gs_ref, 4, whole, d_pre)
    dp_ref[:, inner : inner + 2 * LANES] = d_raw.astype(bf16)
    d_log = through[0:1] + lax.dot_general(
        jnp.where(upper, 1.0, 0.0), d_cum, (((1,), (0,)), ((), ())), precision=highest,
        preferred_element_type=f32,
    )
    rate = rate_ref[...]
    d_raw_step = (d_log * rate + d_direct) * sig_ref[...]
    add_to(gh_ref, 0, whole, d_raw_step)
    add_to(gh_ref, 1, whole, d_log * step * rate)
    dp_ref[:, inner + 2 * LANES :] = d_raw_step.astype(bf16)


def whole_spec(array):
    return pl.BlockSpec(array.shape, lambda c, rot: (0,) * array.ndim)


def scan_forward(rot, p1, pz, step, conv, conv_bias, conv_s, conv_s_bias, rate, skip, gain):
    length, inner = pz.shape
    blocks = length // CHUNK

    def place(width, column=0):
        return pl.BlockSpec((CHUNK, width), lambda c, rot: ((c + rot[0]) % blocks, column))

    params = (conv, conv_bias, conv_s, conv_s_bias, rate, skip, gain)
    return pl.pallas_call(
        forward_kernel,
        grid_spec=pltpu.PrefetchScalarGridSpec(
            num_scalar_prefetch=1,
            grid=(blocks,),
            in_specs=[
                place(inner), place(2 * LANES, inner // (2 * LANES)), place(LANES), place(inner),
                *map(whole_spec, params),
            ],
            out_specs=[
                place(inner),
                pl.BlockSpec((1, 1, CHUNK), lambda c, rot: ((c + rot[0]) % blocks, 0, 0)),
                place(inner),
                pl.BlockSpec((1, LANES, inner), lambda c, rot: (c, 0, 0)),
            ],
            scratch_shapes=[
                pltpu.VMEM((LANES, inner), f32),
                pltpu.VMEM((8, inner), f32),
                pltpu.VMEM((8, 2 * LANES), f32),
            ],
        ),
        out_shape=[
            jax.ShapeDtypeStruct((length, inner), bf16),
            jax.ShapeDtypeStruct((blocks, 1, CHUNK), f32),
            jax.ShapeDtypeStruct((length, inner), f32),
            jax.ShapeDtypeStruct((blocks, LANES, inner), bf16),
        ],
        compiler_params=pltpu.CompilerParams(
            dimension_semantics=("arbitrary",), vmem_limit_bytes=40 * 2**20
        ),
        cost_estimate=pl.CostEstimate(
            flops=int(25e9), bytes_accessed=25 * 2**20, transcendentals=0
        ),
        name="scan_forward",
    )(rot, p1, p1, step, pz, *params)


def scan_backward(rot, p1, pz, step, sig, y, states, d_yn, q, qc, conv, conv_bias, conv_s, conv_s_bias, rate, skip, gain):
    length, inner = pz.shape
    blocks = length // CHUNK

    def place(width, column=0):
        return pl.BlockSpec(
            (CHUNK, width), lambda c, rot: ((blocks - 1 - c + rot[0]) % blocks, column)
        )

    def before(width, column=0):
        return pl.BlockSpec(
            (8, width),
            lambda c, rot: (
                (2 * blocks - 2 - c + rot[0]) % blocks * (CHUNK // 8) + CHUNK // 8 - 1,
                column,
            ),
        )

    def fixed(height, width):
        return pl.BlockSpec((height, width), lambda c, rot: (0, 0))

    line = pl.BlockSpec(
        (1, 1, CHUNK), lambda c, rot: ((blocks - 1 - c + rot[0]) % blocks, 0, 0)
    )
    params = (conv, conv_bias, conv_s, conv_s_bias, rate, skip, gain)
    bc_at = inner // (2 * LANES)
    return pl.pallas_call(
        backward_kernel,
        grid_spec=pltpu.PrefetchScalarGridSpec(
            num_scalar_prefetch=1,
            grid=(blocks,),
            in_specs=[
                place(inner), before(inner), place(2 * LANES, bc_at), before(2 * LANES, bc_at),
                place(LANES), place(LANES), place(inner), place(inner),
                pl.BlockSpec((1, LANES, inner), lambda c, rot: (blocks - 1 - c, 0, 0)),
                place(inner), line, line,
                *map(whole_spec, params),
            ],
            out_specs=[
                place(inner), place(inner + 3 * LANES),
                fixed(8, inner), fixed(8, 2 * LANES), fixed(8, LANES),
            ],
            scratch_shapes=[
                pltpu.VMEM((LANES, inner), f32),
                pltpu.VMEM((LANES, inner), bf16),
                pltpu.VMEM((8, inner), f32),
                pltpu.VMEM((8, 2 * LANES), f32),
                pltpu.VMEM((8, LANES), f32),
            ],
        ),
        out_shape=[
            jax.ShapeDtypeStruct((length, inner), bf16),
            jax.ShapeDtypeStruct((length, inner + 3 * LANES), bf16),
            jax.ShapeDtypeStruct((8, inner), f32),
            jax.ShapeDtypeStruct((8, 2 * LANES), f32),
            jax.ShapeDtypeStruct((8, LANES), f32),
        ],
        compiler_params=pltpu.CompilerParams(
            dimension_semantics=("arbitrary",), vmem_limit_bytes=48 * 2**20
        ),
        cost_estimate=pl.CostEstimate(
            flops=int(45e9), bytes_accessed=40 * 2**20, transcendentals=0
        ),
        name="scan_backward",
    )(rot, p1, p1, p1, p1, step, sig, pz, y, states, d_yn, q, qc, *params)


TENSOR_SWAP = [(0, 1), (1, 0)]


def swap(values):
    return lax.ppermute(values, "tensor", TENSOR_SWAP)


def butterfly(values):
    size = lax.axis_size("dp")
    step = 1
    while step < size:
        values = values + lax.ppermute(values, "dp", [(i, i ^ step) for i in range(size)])
        step *= 2
    return values


def pad_lanes(values):
    return jnp.pad(values, ((0, 0), (0, LANES - values.shape[1])))


def local(
    residual_in, cotangent, input_gain, z_weight, x_weight, bc_weight, dt_weight,
    conv_inner, conv_inner_bias, conv_state, conv_state_bias, dt_bias, decay_log,
    skip_gain, gated_gain, out_weight,
):
    layers = input_gain.shape[0]
    half, width = residual_in.shape
    inner = gated_gain.shape[1]
    heads = dt_bias.shape[1]
    inner_total = inner * lax.axis_size("tensor")
    blocks = 2 * half // CHUNK
    bc_rows = bc_weight.shape[1]
    mine = lax.axis_index("tensor")
    rot = (mine * (blocks // 2)).astype(jnp.int32).reshape(1)

    bc_other = swap(bc_weight)
    bc_pair = jnp.where(
        mine == 0,
        jnp.concatenate([bc_weight, bc_other], axis=1),
        jnp.concatenate([bc_other, bc_weight], axis=1),
    )

    def gather(shard):
        return lax.all_gather(shard, "dp", axis=0, tiled=True)

    weights = []
    for l in range(layers):
        first = jnp.concatenate([x_weight[l], bc_pair[l], pad_lanes(dt_weight[l])], axis=1)
        weights.append((gather(first), gather(z_weight[l]), gather(out_weight[l].T)))

    def params_of(l):
        rate = pad_lanes(-jnp.exp(decay_log[l])[None])
        return (
            conv_inner[l], conv_inner_bias[l][None], conv_state[l], conv_state_bias[l][None],
            rate, jnp.repeat(skip_gain[l], HEADDIM)[None], gated_gain[l][None],
        )

    saved = []
    hidden = residual_in
    for l in range(layers):
        w_first, w_z, w_out = weights[l]
        scale = lax.rsqrt(jnp.mean(hidden * hidden, axis=1, keepdims=True) + epsilon)
        normed = (hidden * scale * input_gain[l]).astype(bf16)
        rows = jnp.concatenate([normed, swap(normed)], axis=0)
        p1 = dot_nn(rows, w_first)
        pz = dot_nn(rows, w_z)
        raw_step = p1[:, inner + 2 * LANES :] + pad_lanes(dt_bias[l][None])
        step = jax.nn.softplus(raw_step)
        sig = jax.nn.sigmoid(raw_step)
        params = params_of(l)
        ghat, squares, y, states = scan_forward(rot, p1, pz, step, *params)
        other = swap(squares)
        squares = squares + jnp.concatenate([other[blocks // 2 :], other[: blocks // 2]], axis=0)
        q = lax.rsqrt(squares / inner_total + epsilon)
        q_col = q.reshape(2 * half, 1)
        out = dot_nt(ghat, w_out) * q_col
        branch = out[:half] + swap(out[half:].astype(bf16)).astype(f32)
        saved.append((hidden, scale, rows, p1, pz, step, sig, params, ghat, y, states, q, q_col, out, branch))
        hidden = hidden + branch

    flow = cotangent
    results = [None] * layers
    for l in reversed(range(layers)):
        w_first, w_z, w_out = weights[l]
        hidden_in, scale, rows, p1, pz, step, sig, params, ghat, y, states, q, q_col, out, branch = saved[l]
        flow_low = flow.astype(bf16)
        go = jnp.concatenate([flow_low, swap(flow_low)], axis=0)
        if l == layers - 1:
            part = jnp.sum(go.astype(f32) * out, axis=1).reshape(blocks, 1, CHUNK)
            other = swap(part)
            dots = part + jnp.concatenate([other[blocks // 2 :], other[: blocks // 2]], axis=0)
        else:
            part = jnp.sum(flow_low.astype(f32) * branch, axis=1).reshape(blocks // 2, 1, CHUNK)
            dots = jnp.concatenate([part, swap(part)], axis=0)
        qc = q * q * dots / inner_total
        d_yn = dot_nn(go, w_out)
        dz, dp, gx, gs, gh = scan_backward(rot, p1, pz, step, sig, y, states, d_yn, q, qc, *params)
        d_rows = dot_nt(dp, w_first) + dot_nt(dz, w_z)
        d_normed = d_rows[:half] + swap(d_rows[half:].astype(bf16)).astype(f32)
        g_out = dot_tn((go.astype(f32) * q_col).astype(bf16), ghat)
        g_first = dot_tn(rows, dp)
        g_z = dot_tn(rows, dz)

        def scatter(values):
            return lax.psum_scatter(
                values.astype(bf16), "dp", scatter_dimension=0, tiled=True
            ).astype(f32)

        g_out, g_first, g_z = scatter(g_out), scatter(g_first), scatter(g_z)
        g_bc = g_first[:, inner : inner + 2 * LANES]
        bc_sent = lax.dynamic_slice_in_dim(g_bc, (1 - mine) * bc_rows, bc_rows, 0)
        g_bc = lax.dynamic_slice_in_dim(g_bc, mine * bc_rows, bc_rows, 0) + swap(bc_sent)

        weighted = d_normed * input_gain[l]
        g_gain = jnp.sum(d_normed * hidden_in * scale, axis=0, keepdims=True)
        inner_dot = jnp.sum(weighted * hidden_in, axis=1, keepdims=True)
        flow = flow + scale * weighted - hidden_in * (scale * scale * scale * inner_dot / width)

        shared = jnp.concatenate([gs[:5].reshape(-1), g_gain.reshape(-1)]).reshape(-1, LANES)
        shared = shared + swap(shared)
        small = jnp.concatenate(
            [shared, gx[:7].reshape(-1, LANES), gh[:2].reshape(-1, LANES)], axis=0
        )
        small = butterfly(small).reshape(-1)
        at = 0

        def take(*shape):
            nonlocal at
            size = 1
            for s in shape:
                size *= s
            at += size
            return small[at - size : at].reshape(shape)

        r_cs, r_csb, r_gain = take(4, 2 * LANES), take(2 * LANES), take(width)
        r_ci, r_cib = take(4, inner), take(inner)
        r_skip = jnp.sum(take(heads, HEADDIM), axis=1)
        r_gated = take(inner)
        r_dtb, r_decay = take(LANES)[:heads], take(LANES)[:heads]
        results[l] = (
            r_gain, g_z, g_first[:, :inner], g_bc,
            g_first[:, inner + 2 * LANES : inner + 2 * LANES + heads],
            r_ci, r_cib, r_cs, r_csb, r_dtb, r_decay, r_skip, r_gated, g_out.T,
        )
    return (hidden, flow, *(jnp.stack(parts) for parts in zip(*results)))


def solution(mesh):
    row = P(("dp", "tensor"), None)
    rest = (
        P(), P(None, "dp", "tensor"), P(None, "dp", "tensor"), P(None, ("dp", "tensor"), None),
        P(None, "dp", "tensor"), P(None, None, "tensor"), P(None, "tensor"), P(), P(),
        P(None, "tensor"), P(None, "tensor"), P(None, "tensor"), P(None, "tensor"),
        P(None, "tensor", "dp"),
    )
    specs = (row, row, *rest)
    return jax.shard_map(local, mesh=mesh, in_specs=specs, out_specs=specs, check_vma=False)
```

```python
import jax
import jax.numpy as jnp
from jax import lax
from jax.experimental import pallas as pl
from jax.experimental.pallas import tpu as pltpu
from jax.sharding import PartitionSpec as P

HEADDIM = 64
CHUNK = 128
LANES = 128
epsilon = 1e-05
highest = lax.Precision.HIGHEST
f32 = jnp.float32
bf16 = jnp.bfloat16


def dot_nn(left, right):
    return lax.dot_general(left, right, (((1,), (0,)), ((), ())), preferred_element_type=f32)


def dot_nt(left, right):
    return lax.dot_general(left, right, (((1,), (1,)), ((), ())), preferred_element_type=f32)


def dot_tn(left, right):
    return lax.dot_general(left, right, (((0,), (0,)), ((), ())), preferred_element_type=f32)


def conv_rows(ext, kernel, offset, length):
    total = offset + kernel[0:1] * ext[5 : 5 + length]
    for tap in range(1, 4):
        total = total + kernel[tap : tap + 1] * ext[5 + tap : 5 + tap + length]
    return total


def row_col(size):
    return (
        lax.broadcasted_iota(jnp.int32, (size, size), 0),
        lax.broadcasted_iota(jnp.int32, (size, size), 1),
    )


def decays(dt_ref, rate_ref, lower):
    step = dt_ref[...]
    cum = lax.dot_general(
        lower, step * rate_ref[...], (((1,), (0,)), ((), ())), precision=highest,
        preferred_element_type=f32,
    )
    last = cum[CHUNK - 1 : CHUNK]
    return step, cum, cum.T, last, jnp.exp(cum), jnp.exp(last - cum)


def forward_kernel(
    rot_ref, xr_ref, bcr_ref, dt_ref, zr_ref,
    cw_ref, cb_ref, sw_ref, sb_ref, rate_ref, skip_ref, gain_ref,
    ghat_ref, ssq_ref, y_ref, s_ref,
    state, x_halo, bc_halo,
):
    @pl.when(pl.program_id(0) == 0)
    def _():
        state[...] = jnp.zeros_like(state)
        x_halo[...] = jnp.zeros_like(x_halo)
        bc_halo[...] = jnp.zeros_like(bc_halo)

    rows, cols = row_col(CHUNK)
    causal = rows >= cols
    low_half = cols < HEADDIM
    step, cum, cum_t, last, grow, tail = decays(dt_ref, rate_ref, jnp.where(causal, 1.0, 0.0))
    tail_step = tail * step
    last_grow = jnp.exp(last)
    bc_ext = jnp.concatenate([bc_halo[...], bcr_ref[...]], axis=0)
    bc_halo[...] = bcr_ref[CHUNK - 8 :]
    bc_pre = conv_rows(bc_ext, sw_ref[...], sb_ref[...], CHUNK)
    bc = (bc_pre * jax.nn.sigmoid(bc_pre)).astype(bf16)
    b_low, c_low = bc[:, :LANES], bc[:, LANES:]
    b_turned = b_low.astype(f32).T.astype(bf16)
    mix = jnp.where(causal, dot_nt(c_low, b_low), 0.0)
    squares = jnp.zeros((CHUNK, LANES), f32)

    def spread(cols_of, head):
        return jnp.where(low_half, cols_of[:, head : head + 1], cols_of[:, head + 1 : head + 2])

    for pair in range(xr_ref.shape[1] // LANES):
        at = slice(pair * LANES, (pair + 1) * LANES)
        head = 2 * pair
        xr = xr_ref[:, at]
        ext = jnp.concatenate([x_halo[:, at], xr], axis=0)
        x_halo[:, at] = xr[CHUNK - 8 :]
        pre = conv_rows(ext, cw_ref[:, at], cb_ref[:, at], CHUNK)
        x = (pre * jax.nn.sigmoid(pre)).astype(bf16).astype(f32)
        x_step = (x * spread(step, head)).astype(bf16)
        s_in = state[:, at]
        s_low = s_in.astype(bf16)
        s_ref[0, :, at] = s_low
        parts = []
        for h in (head, head + 1):
            decay = jnp.exp(jnp.minimum(cum[:, h : h + 1] - cum_t[h : h + 1, :], 0.0))
            parts.append(dot_nn((mix * decay).astype(bf16), x_step))
        across = dot_nn(c_low, s_low) * spread(grow, head)
        y = jnp.where(low_half, parts[0], parts[1]) + across + skip_ref[:, at] * x
        y_ref[:, at] = y
        z = zr_ref[:, at]
        gated = y * (z * jax.nn.sigmoid(z))
        squares = squares + gated * gated
        ghat_ref[:, at] = (gated * gain_ref[:, at]).astype(bf16)
        fresh = dot_nn(b_turned, (x * spread(tail_step, head)).astype(bf16))
        state[:, at] = s_in * spread(last_grow, head)[0:1] + fresh
    ssq_ref[0] = jnp.sum(squares.T, axis=0, keepdims=True)


def backward_kernel(
    rot_ref, xr_ref, xp_ref, bcr_ref, bcp_ref, dt_ref, sig_ref, zr_ref, y_ref, s_ref, dyn_ref, q_ref, qc_ref,
    cw_ref, cb_ref, sw_ref, sb_ref, rate_ref, skip_ref, gain_ref,
    dp_ref, gx_ref, gs_ref, gh_ref,
    dstate, x_halo, bc_halo,
):
    inner = xr_ref.shape[1]
    first = pl.program_id(0) == pl.num_programs(0) - 1

    @pl.when(pl.program_id(0) == 0)
    def _():
        dstate[...] = jnp.zeros_like(dstate)
        x_halo[...] = jnp.zeros_like(x_halo)
        bc_halo[...] = jnp.zeros_like(bc_halo)
        gx_ref[...] = jnp.zeros_like(gx_ref)
        gs_ref[...] = jnp.zeros_like(gs_ref)
        gh_ref[...] = jnp.zeros_like(gh_ref)

    rows, cols = row_col(CHUNK)
    upper = cols >= rows
    low_half = cols < HEADDIM
    keep = jnp.where(first, 0.0, 1.0)
    step, cum, cum_t, last, grow, tail = decays(dt_ref, rate_ref, jnp.where(rows >= cols, 1.0, 0.0))
    tail_step = tail * step
    last_grow = jnp.exp(last)
    bcr = bcr_ref[...]
    bc_ext = jnp.concatenate([bcp_ref[...] * keep, bcr], axis=0)
    bc_pre = conv_rows(bc_ext, sw_ref[...], sb_ref[...], CHUNK)
    bc_sig = jax.nn.sigmoid(bc_pre)
    bc = (bc_pre * bc_sig).astype(bf16)
    b_low, c_low = bc[:, :LANES], bc[:, LANES:]
    c_turned = c_low.astype(f32).T.astype(bf16)
    mix = jnp.where(upper, dot_nt(b_low, c_low), 0.0)
    q = jnp.broadcast_to(q_ref[0], (CHUNK, CHUNK)).T
    qc = jnp.broadcast_to(qc_ref[0], (CHUNK, CHUNK)).T

    def spread(cols_of, head):
        return jnp.where(low_half, cols_of[:, head : head + 1], cols_of[:, head + 1 : head + 2])

    def two_parts(values):
        high = values.astype(bf16)
        return jnp.concatenate([high, (values - high.astype(f32)).astype(bf16)], axis=1)

    def add_to(ref, index, at, values):
        ref[index : index + 1, at] += jnp.sum(values, axis=0, keepdims=True)

    d_mix = jnp.zeros((CHUNK, CHUNK), f32)
    d_b = jnp.zeros((CHUNK, LANES), f32)
    d_c = jnp.zeros((CHUNK, LANES), f32)
    d_cum = jnp.zeros((CHUNK, LANES), f32)
    d_within = jnp.zeros((CHUNK, LANES), f32)
    d_beyond = jnp.zeros((CHUNK, LANES), f32)
    through = jnp.zeros((8, LANES), f32)
    sel_rows = lax.broadcasted_iota(jnp.int32, (2 * LANES, LANES), 0)
    sel_cols = lax.broadcasted_iota(jnp.int32, (2 * LANES, LANES), 1)
    sel_head = jnp.where(sel_rows % LANES < HEADDIM, 0, 1)
    for pair in range(inner // LANES):
        at = slice(pair * LANES, (pair + 1) * LANES)
        head = 2 * pair
        select = jnp.where(sel_cols == sel_head + head, 1.0, 0.0).astype(bf16)
        xr = xr_ref[:, at]
        ext = jnp.concatenate([xp_ref[:, at] * keep, xr], axis=0)
        pre = conv_rows(ext, cw_ref[:, at], cb_ref[:, at], CHUNK)
        sig = jax.nn.sigmoid(pre)
        x_low = (pre * sig).astype(bf16)
        x = x_low.astype(f32)
        step_wide = spread(step, head)
        x_step = (x * step_wide).astype(bf16)
        z = zr_ref[:, at]
        z_sig = jax.nn.sigmoid(z)
        z_act = z * z_sig
        y = y_ref[:, at]
        gated = y * z_act
        dyn = dyn_ref[:, at]
        add_to(gx_ref, 6, at, dyn * gated * q)
        d_gated = dyn * (gain_ref[:, at] * q) - gated * qc
        dp_ref[:, at] = (d_gated * y * (z_sig * (1.0 + z * (1.0 - z_sig)))).astype(bf16)
        dy = d_gated * z_act
        dy_low = dy.astype(bf16)
        dy_wide = dy_low.astype(f32)
        add_to(gx_ref, 5, at, dy * x)
        ds = dstate[:, at]
        ds_low = ds.astype(bf16)
        parts = []
        zero = jnp.zeros_like(x_step)
        for h in (head, head + 1):
            decay = jnp.exp(jnp.minimum(cum_t[h : h + 1, :] - cum[:, h : h + 1], 0.0))
            parts.append(dot_nn((mix * decay).astype(bf16), dy_low))
            own = jnp.where(low_half, x_step, zero) if h == head else jnp.where(low_half, zero, x_step)
            d_mix = d_mix + dot_nt(own, dy_low) * decay
        within = jnp.where(low_half, parts[0], parts[1])
        beyond = dot_nn(b_low, ds_low) * spread(tail, head)
        skip = skip_ref[:, at]
        dx = step_wide * (within + beyond) + skip * dy
        d_cum = d_cum + dot_nn(
            two_parts(dy_wide * (y - skip * x) - x_step.astype(f32) * within), select
        )
        d_within = d_within + dot_nn(two_parts(x * within), select)
        d_beyond = d_beyond + dot_nn(two_parts(x * beyond), select)
        s_low = s_ref[0, :, at]
        crossing = jnp.sum(ds * s_low.astype(f32), axis=0, keepdims=True)
        through = through + dot_nn(two_parts(jnp.broadcast_to(crossing, (8, LANES))), select)
        dy_grow = (dy_wide * spread(grow, head)).astype(bf16)
        d_c = d_c + dot_nt(dy_grow, s_low)
        d_b = d_b + dot_nt((x * spread(tail_step, head)).astype(bf16), ds_low)
        dstate[:, at] = ds * spread(last_grow, head)[0:1] + dot_nn(c_turned, dy_grow)
        d_pre = dx * (sig * (1.0 + pre * (1.0 - sig)))
        d_ext = jnp.concatenate([d_pre, x_halo[:, at]], axis=0)
        x_halo[:, at] = d_pre[:8]
        d_raw = cw_ref[3:4, at] * d_pre
        for tap in range(3):
            d_raw = d_raw + cw_ref[tap : tap + 1, at] * d_ext[3 - tap : 3 - tap + CHUNK]
            add_to(gx_ref, tap, at, d_pre * ext[5 + tap : 5 + tap + CHUNK])
        add_to(gx_ref, 3, at, d_pre * xr)
        add_to(gx_ref, 4, at, d_pre)
        dp_ref[:, inner + at.start : inner + at.stop] = d_raw.astype(bf16)
    d_mix = jnp.where(upper, d_mix, 0.0)
    d_b = d_b + dot_nn(d_mix.astype(bf16), c_low)
    d_c = d_c + dot_nn(d_mix.T.astype(bf16), b_low)
    d_bc = jnp.concatenate([d_b, d_c], axis=1)
    d_pre = d_bc * (bc_sig * (1.0 + bc_pre * (1.0 - bc_sig)))
    d_ext = jnp.concatenate([d_pre, bc_halo[...]], axis=0)
    bc_halo[...] = d_pre[:8]
    d_raw = sw_ref[3:4] * d_pre
    whole = slice(None)
    for tap in range(3):
        d_raw = d_raw + sw_ref[tap : tap + 1] * d_ext[3 - tap : 3 - tap + CHUNK]
        add_to(gs_ref, tap, whole, d_pre * bc_ext[5 + tap : 5 + tap + CHUNK])
    add_to(gs_ref, 3, whole, d_pre * bcr)
    add_to(gs_ref, 4, whole, d_pre)
    dp_ref[:, 2 * inner : 2 * inner + 2 * LANES] = d_raw.astype(bf16)
    d_log = through[0:1] * last_grow + lax.dot_general(
        jnp.concatenate([jnp.where(upper, 1.0, 0.0), jnp.where(upper, 0.0, 1.0)], axis=1),
        jnp.concatenate([d_cum, step * d_beyond], axis=0),
        (((1,), (0,)), ((), ())), precision=highest, preferred_element_type=f32,
    )
    rate = rate_ref[...]
    d_raw_step = (d_log * rate + d_within + d_beyond) * sig_ref[...]
    add_to(gh_ref, 0, whole, d_raw_step)
    add_to(gh_ref, 1, whole, d_log * step * rate)
    dp_ref[:, 2 * inner + 2 * LANES :] = d_raw_step.astype(bf16)


def whole_spec(array):
    return pl.BlockSpec(array.shape, lambda c, rot: (0,) * array.ndim)


def scan_forward(rot, zs, first, first_at, step, conv, conv_bias, conv_s, conv_s_bias, rate, skip, gain):
    length, inner = zs.shape[0], gain.shape[1]
    blocks = length // CHUNK

    def place(width, column=0):
        return pl.BlockSpec((CHUNK, width), lambda c, rot: ((c + rot[0]) % blocks, column))

    params = (conv, conv_bias, conv_s, conv_s_bias, rate, skip, gain)
    return pl.pallas_call(
        forward_kernel,
        grid_spec=pltpu.PrefetchScalarGridSpec(
            num_scalar_prefetch=1,
            grid=(blocks,),
            in_specs=[
                place(inner, first_at // inner), place(2 * LANES, (first_at + inner) // (2 * LANES)), place(LANES), place(inner),
                *map(whole_spec, params),
            ],
            out_specs=[
                place(inner),
                pl.BlockSpec((1, 1, CHUNK), lambda c, rot: ((c + rot[0]) % blocks, 0, 0)),
                place(inner),
                pl.BlockSpec((1, LANES, inner), lambda c, rot: (c, 0, 0)),
            ],
            scratch_shapes=[
                pltpu.VMEM((LANES, inner), f32),
                pltpu.VMEM((8, inner), f32),
                pltpu.VMEM((8, 2 * LANES), f32),
            ],
        ),
        out_shape=[
            jax.ShapeDtypeStruct((length, inner), bf16),
            jax.ShapeDtypeStruct((blocks, 1, CHUNK), f32),
            jax.ShapeDtypeStruct((length, inner), f32),
            jax.ShapeDtypeStruct((blocks, LANES, inner), bf16),
        ],
        compiler_params=pltpu.CompilerParams(
            dimension_semantics=("arbitrary",), vmem_limit_bytes=20 * 2**20
        ),
        cost_estimate=pl.CostEstimate(
            flops=int(25e9), bytes_accessed=25 * 2**20, transcendentals=0
        ),
        name="scan_forward",
    )(rot, first, first, step, zs, *params)


def scan_backward(
    rot, zs, first, first_at, step, sig, y, states, d_yn, q, qc,
    conv, conv_bias, conv_s, conv_s_bias, rate, skip, gain,
):
    length, inner = zs.shape[0], gain.shape[1]
    blocks = length // CHUNK

    def place(width, column=0):
        return pl.BlockSpec(
            (CHUNK, width), lambda c, rot: ((blocks - 1 - c + rot[0]) % blocks, column)
        )

    def before(width, column=0):
        return pl.BlockSpec(
            (8, width),
            lambda c, rot: (
                (2 * blocks - 2 - c + rot[0]) % blocks * (CHUNK // 8) + CHUNK // 8 - 1,
                column,
            ),
        )

    def fixed(height, width):
        return pl.BlockSpec((height, width), lambda c, rot: (0, 0))

    line = pl.BlockSpec(
        (1, 1, CHUNK), lambda c, rot: ((blocks - 1 - c + rot[0]) % blocks, 0, 0)
    )
    params = (conv, conv_bias, conv_s, conv_s_bias, rate, skip, gain)
    x_at, bc_at = first_at // inner, (first_at + inner) // (2 * LANES)
    return pl.pallas_call(
        backward_kernel,
        grid_spec=pltpu.PrefetchScalarGridSpec(
            num_scalar_prefetch=1,
            grid=(blocks,),
            in_specs=[
                place(inner, x_at), before(inner, x_at), place(2 * LANES, bc_at), before(2 * LANES, bc_at),
                place(LANES), place(LANES), place(inner), place(inner),
                pl.BlockSpec((1, LANES, inner), lambda c, rot: (blocks - 1 - c, 0, 0)),
                place(inner), line, line,
                *map(whole_spec, params),
            ],
            out_specs=[
                place(2 * inner + 3 * LANES),
                fixed(8, inner), fixed(8, 2 * LANES), fixed(8, LANES),
            ],
            scratch_shapes=[
                pltpu.VMEM((LANES, inner), f32),
                pltpu.VMEM((8, inner), f32),
                pltpu.VMEM((8, 2 * LANES), f32),
            ],
        ),
        out_shape=[
            jax.ShapeDtypeStruct((length, 2 * inner + 3 * LANES), bf16),
            jax.ShapeDtypeStruct((8, inner), f32),
            jax.ShapeDtypeStruct((8, 2 * LANES), f32),
            jax.ShapeDtypeStruct((8, LANES), f32),
        ],
        compiler_params=pltpu.CompilerParams(
            dimension_semantics=("arbitrary",), vmem_limit_bytes=28 * 2**20
        ),
        cost_estimate=pl.CostEstimate(
            flops=int(45e9), bytes_accessed=40 * 2**20, transcendentals=0
        ),
        name="scan_backward",
    )(rot, first, first, first, first, step, sig, zs, y, states, d_yn, q, qc, *params)


TENSOR_SWAP = [(0, 1), (1, 0)]


def swap(values):
    return lax.ppermute(values, "tensor", TENSOR_SWAP)


def butterfly(values):
    size = lax.axis_size("dp")
    step = 1
    while step < size:
        values = values + lax.ppermute(values, "dp", [(i, i ^ step) for i in range(size)])
        step *= 2
    return values


LINE, SIDE, CORE = 4, 2, 2
PLACES = [(z, x, c) for z in range(LINE) for x in range(SIDE) for c in range(CORE)]


def index_of(z, x, c):
    return (z * SIDE + x) * CORE + c


def along_line(step, lowest, highest_place):
    return [
        (index_of(z, x, c), index_of(z + step, x, c))
        for z, x, c in PLACES
        if lowest <= z <= highest_place
    ]


OTHER_SIDE = [(index_of(z, x, c), index_of(z, 1 - x, c)) for z, x, c in PLACES]
OTHER_CORE = [(index_of(z, x, c), index_of(z, x, 1 - c)) for z, x, c in PLACES]
LINES = [[index_of(z, x, c) for z in range(LINE)] for x in range(SIDE) for c in range(CORE)]


def place_of():
    at = lax.axis_index("dp")
    return at // (SIDE * CORE), (at // CORE) % SIDE, at % CORE


def paired(own, other, mine, axis):
    return jnp.where(
        mine == 0, jnp.stack([own, other], axis=axis), jnp.stack([other, own], axis=axis)
    )


def gather_start(shard):
    if lax.axis_size("dp") != LINE * SIDE * CORE:
        return lax.all_gather(shard, "dp", axis=0, tiled=True)
    z, x, _ = place_of()
    rows, columns = shard.shape
    right, left = [shard], [shard]
    for step in range(1, LINE):
        right.append(lax.ppermute(right[-1], "dp", along_line(1, step - 1, LINE - 2)))
        left.append(lax.ppermute(left[-1], "dp", along_line(-1, 1, LINE - step)))
    line = jnp.concatenate(right[:0:-1] + left, axis=0)
    line = lax.dynamic_slice_in_dim(line, (LINE - 1 - z) * rows, LINE * rows, 0)
    line = line.reshape(LINE, rows, columns)
    return paired(line, lax.ppermute(line, "dp", OTHER_SIDE), x, 1)


def gather_end(pair):
    if lax.axis_size("dp") != LINE * SIDE * CORE:
        return pair
    full = paired(pair, lax.ppermute(pair, "dp", OTHER_CORE), place_of()[2], 2)
    return full.reshape(-1, full.shape[-1])


def part_of(blocks, at, axis):
    return lax.dynamic_index_in_dim(blocks, at, axis, keepdims=False)


def added(kept, got):
    return (kept.astype(f32) + got.astype(f32)).astype(bf16)


def scatter_start(*values):
    if lax.axis_size("dp") != LINE * SIDE * CORE:
        return jnp.concatenate(values, axis=1)
    c = place_of()[2]
    blocks = [v.reshape(LINE, SIDE, CORE, -1, v.shape[1]) for v in values]
    sent = jnp.concatenate([part_of(b, 1 - c, 2) for b in blocks], axis=-1)
    kept = jnp.concatenate([part_of(b, c, 2) for b in blocks], axis=-1)
    return added(kept, lax.ppermute(sent, "dp", OTHER_CORE))


def scatter_middle(blocks):
    if lax.axis_size("dp") != LINE * SIDE * CORE:
        return blocks
    x = place_of()[1]
    got = lax.ppermute(part_of(blocks, 1 - x, 1), "dp", OTHER_SIDE)
    return added(part_of(blocks, x, 1), got)


def scatter_end(blocks):
    if lax.axis_size("dp") != LINE * SIDE * CORE:
        return scatter_plain(blocks)
    return lax.psum_scatter(
        blocks.reshape(-1, blocks.shape[-1]), "dp", scatter_dimension=0, tiled=True,
        axis_index_groups=LINES,
    )


def after(values, *earlier):
    return lax.optimization_barrier((values, *earlier))[0]


def gather_plain(shard):
    return lax.all_gather(shard, "dp", axis=0, tiled=True)


def scatter_plain(values):
    return lax.psum_scatter(values, "dp", scatter_dimension=0, tiled=True)


def rolled(values):
    half = values.shape[0] // 2
    return jnp.concatenate([values[half:], values[:half]], axis=0)


def pad_lanes(values):
    return jnp.pad(values, ((0, 0), (0, LANES - values.shape[1])))


def local(
    residual_in, cotangent, input_gain, z_weight, x_weight, bc_weight, dt_weight,
    conv_inner, conv_inner_bias, conv_state, conv_state_bias, dt_bias, decay_log,
    skip_gain, gated_gain, out_weight,
):
    layers = input_gain.shape[0]
    half, width = residual_in.shape
    inner = gated_gain.shape[1]
    heads = dt_bias.shape[1]
    inner_total = inner * lax.axis_size("tensor")
    blocks = 2 * half // CHUNK
    bc_rows = bc_weight.shape[1]
    mine = lax.axis_index("tensor")
    rot = (mine * (blocks // 2)).astype(jnp.int32).reshape(1)

    bc_other = swap(bc_weight)
    bc_pair = jnp.where(
        mine == 0,
        jnp.concatenate([bc_weight, bc_other], axis=1),
        jnp.concatenate([bc_other, bc_weight], axis=1),
    )

    def first_shard(l):
        return jnp.concatenate([x_weight[l], bc_pair[l], pad_lanes(dt_weight[l])], axis=1)

    def project(rows, l):
        if l == 0:
            pair, w_first, w_out = weights[0]
            first = dot_nn(rows, w_first)
            w_z = gather_end(after(pair, first))
            weights[0] = (w_z, w_first, w_out)
            return dot_nn(rows, w_z), first, 0
        both = dot_nn(rows, weights[l][0])
        return both, both, inner

    def project_back(d_proj, l):
        if l == 0:
            w_z, w_first, _ = weights[l]
            return dot_nt(d_proj[:, :inner], w_z) + dot_nt(d_proj[:, inner:], w_first)
        return dot_nt(d_proj, weights[l][0])

    weights = [(gather_start(z_weight[0]), gather_plain(first_shard(0)), gather_plain(out_weight[0].T))]
    for l in range(1, layers):
        both = jnp.concatenate([z_weight[l], first_shard(l)], axis=1)
        weights.append((gather_plain(both), gather_plain(out_weight[l].T)))

    def params_of(l):
        rate = pad_lanes(-jnp.exp(decay_log[l])[None])
        return (
            conv_inner[l], conv_inner_bias[l][None], conv_state[l], conv_state_bias[l][None],
            rate, jnp.repeat(skip_gain[l], HEADDIM)[None], gated_gain[l][None],
        )

    saved = []
    hidden = residual_in
    for l in range(layers):
        w_out = weights[l][-1]
        scale = lax.rsqrt(jnp.mean(hidden * hidden, axis=1, keepdims=True) + epsilon)
        normed = (hidden * scale * input_gain[l]).astype(bf16)
        rows = jnp.concatenate([normed, swap(normed)], axis=0)
        zs, first, first_at = project(rows, l)
        raw_step = first[:, first_at + inner + 2 * LANES :] + pad_lanes(dt_bias[l][None])
        step = jax.nn.softplus(raw_step)
        sig = jax.nn.sigmoid(raw_step)
        params = params_of(l)
        ghat, squares, y, states = scan_forward(rot, zs, first, first_at, step, *params)
        squares = squares + rolled(swap(squares))
        q = lax.rsqrt(squares / inner_total + epsilon)
        q_col = q.reshape(2 * half, 1)
        out = dot_nt(ghat, w_out) * q_col
        out_sent = out[half:].astype(bf16)
        dots = None
        if l == layers - 1:
            flow_low = cotangent.astype(bf16)
            go = jnp.concatenate([flow_low, swap(flow_low)], axis=0)
            part = jnp.sum(go.astype(f32) * out, axis=1).reshape(blocks, 1, CHUNK)
            other = swap(part)
            dots = part + rolled(other)
            out_sent = after(out_sent, other)
        branch = out[:half] + swap(out_sent).astype(f32)
        saved.append((hidden, scale, rows, zs, first, first_at, step, sig, params, ghat, y, states, q, q_col, branch))
        hidden = hidden + branch

    flow = cotangent
    summed = []
    large, early, late = [None] * layers, [None] * layers, [None] * layers
    for l in reversed(range(layers)):
        w_out = weights[l][-1]
        (
            hidden_in, scale, rows, zs, first, first_at, step, sig, params, ghat, y, states, q, q_col,
            branch,
        ) = saved[l]
        if l < layers - 1:
            flow_low = flow.astype(bf16)
            part = jnp.sum(flow_low.astype(f32) * branch, axis=1).reshape(blocks // 2, 1, CHUNK)
            dots = jnp.concatenate([part, swap(part)], axis=0)
            go = jnp.concatenate([flow_low, swap(flow_low)], axis=0)
        qc = q * q * dots / inner_total
        go_scaled = (go.astype(f32) * q_col).astype(bf16)
        if l == 0:
            g_out = dot_tn(go_scaled, ghat).astype(bf16)
            d_yn = dot_nn(go, w_out)
            z_sig = jax.nn.sigmoid(zs)
            d_gated = d_yn * params[-1] * q_col - y * (zs * z_sig) * qc.reshape(2 * half, 1)
            dz = (d_gated * y * (z_sig * (1.0 + zs * (1.0 - z_sig)))).astype(bf16)
            g_pair = scatter_start(g_out, dot_tn(rows, dz).astype(bf16))
            d_yn, g_pair = lax.optimization_barrier((d_yn, g_pair))
            g_pair = scatter_middle(g_pair)
        else:
            d_yn = dot_nn(go, w_out)
        d_proj, gx, gs, gh = scan_backward(
            rot, zs, first, first_at, step, sig, y, states, d_yn, q, qc, *params
        )
        if l == 0:
            d_proj, *_ = lax.optimization_barrier((d_proj, *summed))
            g_first = dot_tn(rows, d_proj[:, inner:]).astype(bf16)
            d_proj, g_first = lax.optimization_barrier((d_proj, g_first))
            g_first = scatter_start(g_first)
        d_rows = project_back(d_proj, l)
        d_sent = d_rows[half:].astype(bf16)
        if l == layers - 1:
            d_sent, hidden = lax.optimization_barrier((d_sent, hidden))
        if l == 0:
            d_sent, g_first = lax.optimization_barrier((d_sent, g_first))
        d_got = swap(d_sent)
        if l == 0:
            g_first = scatter_middle(g_first)
            d_got, g_first = lax.optimization_barrier((d_got, g_first))
            g_first = scatter_end(g_first).astype(f32)
            g_pair = scatter_end(g_pair).astype(f32)
            g_out, g_z = g_pair[:, :inner], g_pair[:, inner:]
        else:
            go_scaled, d_proj, _ = lax.optimization_barrier((go_scaled, d_proj, d_sent))
            g_all = jnp.concatenate(
                [dot_tn(rows, d_proj).astype(bf16), dot_tn(go_scaled, ghat).astype(bf16)], axis=1
            )
            d_got, g_all = lax.optimization_barrier((d_got, g_all))
            g_all = scatter_plain(g_all)
            summed.append(g_all)
            g_all = g_all.astype(f32)
            g_z, g_first, g_out = (
                g_all[:, :inner], g_all[:, inner : -inner], g_all[:, -inner:],
            )
        d_normed = d_rows[:half] + d_got.astype(f32)
        g_bc = g_first[:, inner : inner + 2 * LANES]
        bc_sent = lax.dynamic_slice_in_dim(g_bc, (1 - mine) * bc_rows, bc_rows, 0)
        g_bc = lax.dynamic_slice_in_dim(g_bc, mine * bc_rows, bc_rows, 0) + swap(bc_sent)

        weighted = d_normed * input_gain[l]
        g_gain = jnp.sum(d_normed * hidden_in * scale, axis=0).reshape(-1, LANES)
        inner_dot = jnp.sum(weighted * hidden_in, axis=1, keepdims=True)
        flow = flow + scale * weighted - hidden_in * (scale * scale * scale * inner_dot / width)
        large[l] = (
            g_z, g_first[:, :inner], g_bc,
            g_first[:, inner + 2 * LANES : inner + 2 * LANES + heads], g_out.T,
        )
        early[l] = (gs[:5].reshape(-1, LANES), gx[:7].reshape(-1, LANES), gh[:2])
        late[l] = g_gain

    shared = jnp.concatenate([e[0] for e in early] + late, axis=0)
    shared = shared + swap(shared)
    small = butterfly(jnp.concatenate([shared] + [part for e in early for part in e[1:]], axis=0))
    at = 0

    def take(*shape):
        nonlocal at
        size = 1
        for s in shape:
            size *= s
        at += size // LANES
        return small[at - size // LANES : at].reshape(shape)

    r_state = jnp.stack([take(5, 2 * LANES) for _ in range(layers)])
    r_gain = jnp.stack([take(width) for _ in range(layers)])
    r_inner, r_head = zip(*[(take(7, inner), take(2, LANES)) for _ in range(layers)])
    r_inner, r_head = jnp.stack(r_inner), jnp.stack(r_head)[:, :, :heads]
    g_z, g_x, g_bc, g_dt, g_out = (jnp.stack(parts) for parts in zip(*large))
    return (
        hidden, flow, r_gain, g_z, g_x, g_bc, g_dt,
        r_inner[:, :4], r_inner[:, 4], r_state[:, :4], r_state[:, 4],
        r_head[:, 0], r_head[:, 1],
        jnp.sum(r_inner[:, 5].reshape(layers, heads, HEADDIM), axis=2), r_inner[:, 6], g_out,
    )


def solution(mesh):
    row = P(("dp", "tensor"), None)
    rest = (
        P(), P(None, "dp", "tensor"), P(None, "dp", "tensor"), P(None, ("dp", "tensor"), None),
        P(None, "dp", "tensor"), P(None, None, "tensor"), P(None, "tensor"), P(), P(),
        P(None, "tensor"), P(None, "tensor"), P(None, "tensor"), P(None, "tensor"),
        P(None, "tensor", "dp"),
    )
    specs = (row, row, *rest)
    return jax.shard_map(local, mesh=mesh, in_specs=specs, out_specs=specs, check_vma=False)
```

```python
import functools

import jax
import jax.numpy as jnp
from jax import lax
from jax.experimental import pallas as pl
from jax.experimental.pallas import tpu as pltpu
from jax.sharding import PartitionSpec as P

HEADDIM = 64
CHUNK = 128
LANES = 128
WIDE = 256
epsilon = 1e-05
f32 = jnp.float32
bf16 = jnp.bfloat16


def dot_nn(left, right):
    return lax.dot_general(left, right, (((1,), (0,)), ((), ())), preferred_element_type=f32)


def dot_nt(left, right):
    return lax.dot_general(left, right, (((1,), (1,)), ((), ())), preferred_element_type=f32)


def dot_tn(left, right):
    return lax.dot_general(left, right, (((0,), (0,)), ((), ())), preferred_element_type=f32)


def conv_rows(ext, kernel, offset, length):
    total = offset + kernel[0:1] * ext[5 : 5 + length]
    for tap in range(1, 4):
        total = total + kernel[tap : tap + 1] * ext[5 + tap : 5 + tap + length]
    return total


def row_col(size):
    return (
        lax.broadcasted_iota(jnp.int32, (size, size), 0),
        lax.broadcasted_iota(jnp.int32, (size, size), 1),
    )


def decays(dt_ref, rate_ref, lower):
    step = dt_ref[...]
    lower = lower.astype(bf16)
    cum = dot_nn(jnp.concatenate([lower] * 3, axis=1), three_parts(step * rate_ref[...]))
    last = cum[CHUNK - 1 : CHUNK]
    return step, cum, cum.T, last, jnp.exp(cum), jnp.exp(last - cum)


def two_parts(values, axis):
    high = values.astype(bf16)
    return jnp.concatenate([high, (values - high.astype(f32)).astype(bf16)], axis=axis)


def three_parts(values):
    high = values.astype(bf16)
    rest = values - high.astype(f32)
    middle = rest.astype(bf16)
    return jnp.concatenate([high, middle, (rest - middle.astype(f32)).astype(bf16)], axis=0)


def heads_of(channels, axis):
    shape = (channels, LANES) if axis == 0 else (LANES, channels)
    at = lax.broadcasted_iota(jnp.int32, shape, axis)
    head = lax.broadcasted_iota(jnp.int32, shape, 1 - axis)
    return jnp.where((at >= head * HEADDIM) & (at < (head + 1) * HEADDIM), 1.0, 0.0).astype(bf16)


def block_diagonal(values, low_half):
    zero = jnp.zeros_like(values)
    return jnp.concatenate(
        [jnp.where(low_half, values, zero), jnp.where(low_half, zero, values)], axis=0
    )


def forward_kernel(
    rot_ref, xr_ref, bcr_ref, dt_ref, zr_ref,
    cw_ref, cb_ref, sw_ref, sb_ref, rate_ref, skip_ref, gain_ref,
    ghat_ref, ssq_ref, y_ref, s_ref, pre_ref, bc_pre_ref,
    state, x_halo, bc_halo, widen, wide,
):
    @pl.when(pl.program_id(0) == 0)
    def _():
        widen[...] = jnp.concatenate([heads_of(xr_ref.shape[1], 1)] * 2, axis=0)
        state[...] = jnp.zeros_like(state)
        x_halo[...] = jnp.zeros_like(x_halo)
        bc_halo[...] = jnp.zeros_like(bc_halo)

    rows, cols = row_col(CHUNK)
    causal = rows >= cols
    low_half = cols < HEADDIM
    step, cum, cum_t, last, grow, tail = decays(dt_ref, rate_ref, jnp.where(causal, 1.0, 0.0))
    wide[...] = dot_nn(two_parts(jnp.concatenate([step, grow, tail], axis=0), 1), widen[...])
    last_grow = jnp.exp(last)
    bc_ext = jnp.concatenate([bc_halo[...], bcr_ref[...]], axis=0)
    bc_halo[...] = bcr_ref[CHUNK - 8 :]
    bc_pre = conv_rows(bc_ext, sw_ref[...], sb_ref[...], CHUNK)
    bc_pre_ref[...] = bc_pre
    bc = (bc_pre * jax.nn.sigmoid(bc_pre)).astype(bf16)
    b_low, c_low = bc[:, :LANES], bc[:, LANES:]
    b_turned = b_low.astype(f32).T.astype(bf16)
    mix = jnp.where(causal, dot_nt(c_low, b_low), 0.0)
    squares = jnp.zeros((CHUNK, LANES), f32)

    def spread(cols_of, quad):
        low = low_half[: cols_of.shape[0]]
        return jnp.concatenate(
            [
                jnp.where(low, cols_of[:, h : h + 1], cols_of[:, h + 1 : h + 2])
                for h in (4 * quad, 4 * quad + 2)
            ],
            axis=1,
        )

    for quad in range(xr_ref.shape[1] // WIDE):
        at = slice(quad * WIDE, (quad + 1) * WIDE)
        xr = xr_ref[:, at]
        ext = jnp.concatenate([x_halo[:, at], xr], axis=0)
        x_halo[:, at] = xr[CHUNK - 8 :]
        pre = conv_rows(ext, cw_ref[:, at], cb_ref[:, at], CHUNK)
        pre_ref[:, at] = pre
        x = (pre * jax.nn.sigmoid(pre)).astype(bf16).astype(f32)
        x_stepped = x * wide[:CHUNK, at]
        x_step = x_stepped.astype(bf16)
        s_in = state[:, at]
        s_low = s_in.astype(bf16)
        s_ref[0, :, at] = s_low
        parts = []
        for pair in range(2):
            mixed = []
            for h in range(4 * quad + 2 * pair, 4 * quad + 2 * pair + 2):
                decay = jnp.exp(jnp.minimum(cum[:, h : h + 1] - cum_t[h : h + 1, :], 0.0))
                mixed.append((mix * decay).astype(bf16))
            right = block_diagonal(x_step[:, pair * LANES : (pair + 1) * LANES], low_half)
            parts.append(dot_nn(jnp.concatenate(mixed, axis=1), right))
        across = dot_nn(c_low, s_low) * wide[CHUNK : 2 * CHUNK, at]
        y = jnp.concatenate(parts, axis=1) + across + skip_ref[:, at] * x
        y_ref[:, at] = y
        z = zr_ref[:, at]
        gated = y * (z * jax.nn.sigmoid(z))
        squared = gated * gated
        squares = squares + (squared[:, :LANES] + squared[:, LANES:])
        ghat_ref[:, at] = (gated * gain_ref[:, at]).astype(bf16)
        fresh = dot_nn(b_turned, (x_stepped * wide[2 * CHUNK :, at]).astype(bf16))
        state[:, at] = s_in * spread(last_grow, quad) + fresh
    ssq_ref[0] = jnp.sum(squares.T, axis=0, keepdims=True)


def backward_kernel(
    gate_at, x_at, rot_ref, xr_ref, pre_ref, bcr_ref, bc_pre_ref, dt_ref, sig_ref, zr_ref, y_ref, s_ref, dyn_ref, q_ref, qc_ref,
    cw_ref, sw_ref, rate_ref, skip_ref, gain_ref,
    dp_ref, gx_ref, gs_ref, gh_ref,
    dstate, x_halo, bc_halo, narrow, products, crossings, gx_parts, gs_parts, gh_parts,
):
    inner = xr_ref.shape[1]
    first = pl.program_id(0) == pl.num_programs(0) - 1

    @pl.when(pl.program_id(0) == 0)
    def _():
        dstate[...] = jnp.zeros_like(dstate)
        x_halo[...] = jnp.zeros_like(x_halo)
        bc_halo[...] = jnp.zeros_like(bc_halo)
        narrow[...] = heads_of(inner, 0)
        gx_parts[...] = jnp.zeros_like(gx_parts)
        gs_parts[...] = jnp.zeros_like(gs_parts)
        gh_parts[...] = jnp.zeros_like(gh_parts)

    rows, cols = row_col(CHUNK)
    upper = cols >= rows
    low_half = cols < HEADDIM
    step, cum, cum_t, last, grow, tail = decays(dt_ref, rate_ref, jnp.where(rows >= cols, 1.0, 0.0))
    last_grow = jnp.exp(last)
    bcr = bcr_ref[...]
    bc_pre = bc_pre_ref[...]
    bc_sig = jax.nn.sigmoid(bc_pre)
    bc = (bc_pre * bc_sig).astype(bf16)
    b_low, c_low = bc[:, :LANES], bc[:, LANES:]
    c_turned = c_low.astype(f32).T.astype(bf16)
    mix = jnp.where(upper, dot_nt(b_low, c_low), 0.0)
    q = jnp.broadcast_to(q_ref[0], (WIDE, CHUNK)).T
    qc = jnp.broadcast_to(qc_ref[0], (WIDE, CHUNK)).T

    def spread(cols_of, quad):
        low = low_half[: cols_of.shape[0]]
        return jnp.concatenate(
            [
                jnp.where(low, cols_of[:, h : h + 1], cols_of[:, h + 1 : h + 2])
                for h in (4 * quad, 4 * quad + 2)
            ],
            axis=1,
        )

    def add_to(parts, index, at, values):
        parts[8 * index : 8 * index + 8, at] += jnp.sum(
            values.reshape(CHUNK // 8, 8, values.shape[1]), axis=0
        )

    d_mix = jnp.zeros((CHUNK, CHUNK), f32)
    d_b = jnp.zeros((CHUNK, LANES), f32)
    d_c = jnp.zeros((CHUNK, LANES), f32)
    for quad in range(inner // WIDE):
        at = slice(quad * WIDE, (quad + 1) * WIDE)
        xr = xr_ref[:, at]
        pre = pre_ref[:, at]
        sig = jax.nn.sigmoid(pre)
        x_low = (pre * sig).astype(bf16)
        x = x_low.astype(f32)
        step_wide = spread(step, quad)
        x_stepped = x * step_wide
        x_step = x_stepped.astype(bf16)
        z = zr_ref[:, at]
        z_sig = jax.nn.sigmoid(z)
        z_act = z * z_sig
        y = y_ref[:, at]
        gated = y * z_act
        dyn = dyn_ref[:, at]
        add_to(gx_parts, 6, at, dyn * gated * q)
        d_gated = dyn * (gain_ref[:, at] * q) - gated * qc
        if gate_at is not None:
            dp_ref[:, at] = (d_gated * y * (z_sig * (1.0 + z * (1.0 - z_sig)))).astype(bf16)
        dy = d_gated * z_act
        dy_low = dy.astype(bf16)
        dy_wide = dy_low.astype(f32)
        add_to(gx_parts, 5, at, dy * x)
        ds = dstate[:, at]
        ds_low = ds.astype(bf16)
        parts = []
        for pair in range(2):
            half = slice(pair * LANES, (pair + 1) * LANES)
            own = [
                jnp.exp(jnp.minimum(cum_t[h : h + 1, :] - cum[:, h : h + 1], 0.0))
                for h in range(4 * quad + 2 * pair, 4 * quad + 2 * pair + 2)
            ]
            right = block_diagonal(dy_low[:, half], low_half)
            mixed = jnp.concatenate([(mix * decay).astype(bf16) for decay in own], axis=1)
            parts.append(dot_nn(mixed, right))
            d_mixed = dot_nt(x_step[:, half], right)
            d_mix = d_mix + d_mixed[:, :CHUNK] * own[0] + d_mixed[:, CHUNK:] * own[1]
        within = jnp.concatenate(parts, axis=1)
        tail_wide = spread(tail, quad)
        beyond = dot_nn(b_low, ds_low) * tail_wide
        skip = skip_ref[:, at]
        dx = step_wide * (within + beyond) + skip * dy
        moved = dy_wide * (y - skip * x) - x_step.astype(f32) * within
        products[: 2 * CHUNK, at] = two_parts(moved, 0)
        products[2 * CHUNK : 3 * CHUNK, at] = (x * within).astype(bf16)
        products[3 * CHUNK :, at] = (x * beyond).astype(bf16)
        s_low = s_ref[0, :, at]
        crossings[:, at] = jnp.sum(
            (ds * s_low.astype(f32)).reshape(CHUNK // 8, 8, WIDE), axis=0
        )
        dy_grow = (dy_wide * spread(grow, quad)).astype(bf16)
        d_c = d_c + dot_nt(dy_grow, s_low)
        d_b = d_b + dot_nt((x_stepped * tail_wide).astype(bf16), ds_low)
        dstate[:, at] = ds * spread(last_grow, quad) + dot_nn(c_turned, dy_grow)
        d_pre = dx * (sig * (1.0 + pre * (1.0 - sig)))
        d_ext = jnp.concatenate([d_pre, x_halo[:, at]], axis=0)
        x_halo[:, at] = d_pre[:8]
        d_raw = cw_ref[3:4, at] * d_pre
        for tap in range(3):
            moved = d_ext[3 - tap : 3 - tap + CHUNK]
            d_raw = d_raw + cw_ref[tap : tap + 1, at] * moved
            add_to(gx_parts, tap, at, moved * xr)
        add_to(gx_parts, 3, at, d_pre * xr)
        add_to(gx_parts, 4, at, d_pre)
        dp_ref[:, x_at + at.start : x_at + at.stop] = d_raw.astype(bf16)
    d_mix = jnp.where(upper, d_mix, 0.0)
    d_b = d_b + dot_nn(d_mix.astype(bf16), c_low)
    d_c = d_c + dot_nn(d_mix.T.astype(bf16), b_low)
    d_bc = jnp.concatenate([d_b, d_c], axis=1)
    d_pre = d_bc * (bc_sig * (1.0 + bc_pre * (1.0 - bc_sig)))
    d_ext = jnp.concatenate([d_pre, bc_halo[...]], axis=0)
    bc_halo[...] = d_pre[:8]
    d_raw = sw_ref[3:4] * d_pre
    whole = slice(None)
    for tap in range(3):
        moved = d_ext[3 - tap : 3 - tap + CHUNK]
        d_raw = d_raw + sw_ref[tap : tap + 1] * moved
        add_to(gs_parts, tap, whole, moved * bcr)
    add_to(gs_parts, 3, whole, d_pre * bcr)
    add_to(gs_parts, 4, whole, d_pre)
    dp_ref[:, x_at + inner : x_at + inner + 2 * LANES] = d_raw.astype(bf16)
    sums = dot_nn(products[...], narrow[...])
    d_cum = sums[:CHUNK] + sums[CHUNK : 2 * CHUNK]
    d_beyond = sums[3 * CHUNK :]
    through = jnp.sum(dot_nn(two_parts(crossings[...], 0), narrow[...]), axis=0, keepdims=True)
    later = jnp.where(upper, 1.0, 0.0).astype(bf16)
    d_log = through * last_grow + dot_nn(
        jnp.concatenate([later] * 3 + [1 - later] * 3, axis=1),
        jnp.concatenate([three_parts(d_cum), three_parts(step * d_beyond)], axis=0),
    )
    rate = rate_ref[...]
    d_raw_step = (d_log * rate + sums[2 * CHUNK : 3 * CHUNK] + d_beyond) * sig_ref[...]
    add_to(gh_parts, 0, whole, d_raw_step)
    add_to(gh_parts, 1, whole, d_log * step * rate)
    dp_ref[:, x_at + inner + 2 * LANES :] = d_raw_step.astype(bf16)

    @pl.when(first)
    def _():
        for parts, ref in ((gx_parts, gx_ref), (gs_parts, gs_ref), (gh_parts, gh_ref)):
            width = ref.shape[1]
            ref[...] = jnp.sum(parts[...].reshape(8, 8, width), axis=1)


def in_hbm(*arrays):
    return [pltpu.with_memory_space_constraint(array, pltpu.HBM) for array in arrays]


def whole_spec(array):
    return pl.BlockSpec(array.shape, lambda c, rot: (0,) * array.ndim)


def scan_forward(rot, zs, first, first_at, step, conv, conv_bias, conv_s, conv_s_bias, rate, skip, gain):
    length, inner = zs.shape[0], gain.shape[1]
    blocks = length // CHUNK

    def place(width, column=0):
        return pl.BlockSpec((CHUNK, width), lambda c, rot: ((c + rot[0]) % blocks, column))

    params = (conv, conv_bias, conv_s, conv_s_bias, rate, skip, gain)
    return pl.pallas_call(
        forward_kernel,
        grid_spec=pltpu.PrefetchScalarGridSpec(
            num_scalar_prefetch=1,
            grid=(blocks,),
            in_specs=[
                place(inner, first_at // inner), place(2 * LANES, (first_at + inner) // (2 * LANES)), place(LANES), place(inner),
                *map(whole_spec, params),
            ],
            out_specs=[
                place(inner),
                pl.BlockSpec((1, 1, CHUNK), lambda c, rot: ((c + rot[0]) % blocks, 0, 0)),
                place(inner),
                pl.BlockSpec((1, LANES, inner), lambda c, rot: (c, 0, 0)),
                place(inner), place(2 * LANES),
            ],
            scratch_shapes=[
                pltpu.VMEM((LANES, inner), f32),
                pltpu.VMEM((8, inner), f32),
                pltpu.VMEM((8, 2 * LANES), f32),
                pltpu.VMEM((2 * LANES, inner), bf16),
                pltpu.VMEM((3 * CHUNK, inner), f32),
            ],
        ),
        out_shape=[
            jax.ShapeDtypeStruct((length, inner), bf16),
            jax.ShapeDtypeStruct((blocks, 1, CHUNK), f32),
            pltpu.HBM((length, inner), f32),
            pltpu.HBM((blocks, LANES, inner), bf16),
            pltpu.HBM((length, inner), f32),
            pltpu.HBM((length, 2 * LANES), f32),
        ],
        compiler_params=pltpu.CompilerParams(
            dimension_semantics=("arbitrary",), vmem_limit_bytes=20 * 2**20
        ),
        cost_estimate=pl.CostEstimate(
            flops=int(25e9), bytes_accessed=25 * 2**20, transcendentals=0
        ),
        name="scan_forward",
    )(rot, *in_hbm(first, first), step, *in_hbm(zs), *params)


def scan_backward(
    rot, with_gate, zs, first, first_at, step, sig, y, states, pre, bc_pre, d_yn, q, qc,
    conv, conv_bias, conv_s, conv_s_bias, rate, skip, gain,
):
    length, inner = zs.shape[0], gain.shape[1]
    blocks = length // CHUNK

    def place(width, column=0):
        return pl.BlockSpec(
            (CHUNK, width), lambda c, rot: ((blocks - 1 - c + rot[0]) % blocks, column)
        )

    def fixed(height, width):
        return pl.BlockSpec((height, width), lambda c, rot: (0, 0))

    line = pl.BlockSpec(
        (1, 1, CHUNK), lambda c, rot: ((blocks - 1 - c + rot[0]) % blocks, 0, 0)
    )
    params = (conv, conv_s, rate, skip, gain)
    x_at, bc_at = first_at // inner, (first_at + inner) // (2 * LANES)
    out_width = (2 if with_gate else 1) * inner + 3 * LANES
    kernel = functools.partial(
        backward_kernel, 0 if with_gate else None, inner if with_gate else 0
    )
    return pl.pallas_call(
        kernel,
        grid_spec=pltpu.PrefetchScalarGridSpec(
            num_scalar_prefetch=1,
            grid=(blocks,),
            in_specs=[
                place(inner, x_at), place(inner), place(2 * LANES, bc_at), place(2 * LANES),
                place(LANES), place(LANES), place(inner), place(inner),
                pl.BlockSpec((1, LANES, inner), lambda c, rot: (blocks - 1 - c, 0, 0)),
                place(inner), line, line,
                *map(whole_spec, params),
            ],
            out_specs=[
                place(out_width),
                fixed(8, inner), fixed(8, 2 * LANES), fixed(8, LANES),
            ],
            scratch_shapes=[
                pltpu.VMEM((LANES, inner), f32),
                pltpu.VMEM((8, inner), f32),
                pltpu.VMEM((8, 2 * LANES), f32),
                pltpu.VMEM((inner, LANES), bf16),
                pltpu.VMEM((4 * CHUNK, inner), bf16),
                pltpu.VMEM((8, inner), f32),
                pltpu.VMEM((64, inner), f32),
                pltpu.VMEM((64, 2 * LANES), f32),
                pltpu.VMEM((64, LANES), f32),
            ],
        ),
        out_shape=[
            jax.ShapeDtypeStruct((length, out_width), bf16),
            jax.ShapeDtypeStruct((8, inner), f32),
            jax.ShapeDtypeStruct((8, 2 * LANES), f32),
            jax.ShapeDtypeStruct((8, LANES), f32),
        ],
        compiler_params=pltpu.CompilerParams(
            dimension_semantics=("arbitrary",), vmem_limit_bytes=28 * 2**20
        ),
        cost_estimate=pl.CostEstimate(
            flops=int(45e9), bytes_accessed=40 * 2**20, transcendentals=0
        ),
        name="scan_backward",
    )(rot, *in_hbm(first, pre, first, bc_pre), step, sig, *in_hbm(zs, y, states, d_yn), q, qc, *params)


TENSOR_SWAP = [(0, 1), (1, 0)]


def swap(values):
    return lax.ppermute(values, "tensor", TENSOR_SWAP)


def butterfly(values):
    size = lax.axis_size("dp")
    step = 1
    while step < size:
        values = values + lax.ppermute(values, "dp", [(i, i ^ step) for i in range(size)])
        step *= 2
    return values


LINE, SIDE, CORE = 4, 2, 2
PLACES = [(z, x, c) for z in range(LINE) for x in range(SIDE) for c in range(CORE)]


def index_of(z, x, c):
    return (z * SIDE + x) * CORE + c


def along_line(step, lowest, highest_place):
    return [
        (index_of(z, x, c), index_of(z + step, x, c))
        for z, x, c in PLACES
        if lowest <= z <= highest_place
    ]


OTHER_SIDE = [(index_of(z, x, c), index_of(z, 1 - x, c)) for z, x, c in PLACES]
OTHER_CORE = [(index_of(z, x, c), index_of(z, x, 1 - c)) for z, x, c in PLACES]
LINES = [[index_of(z, x, c) for z in range(LINE)] for x in range(SIDE) for c in range(CORE)]


def place_of():
    at = lax.axis_index("dp")
    return at // (SIDE * CORE), (at // CORE) % SIDE, at % CORE


def paired(own, other, mine, axis):
    return jnp.where(
        mine == 0, jnp.stack([own, other], axis=axis), jnp.stack([other, own], axis=axis)
    )


def gather_start(shard):
    if lax.axis_size("dp") != LINE * SIDE * CORE:
        return (lax.all_gather(shard, "dp", axis=0, tiled=True),)
    z = place_of()[0]
    rows, columns = shard.shape
    right, left = [shard], [shard]
    for step in range(1, LINE):
        right.append(lax.ppermute(right[-1], "dp", along_line(1, step - 1, LINE - 2)))
        left.append(lax.ppermute(left[-1], "dp", along_line(-1, 1, LINE - step)))
    line = jnp.concatenate(right[:0:-1] + left, axis=0)
    line = lax.dynamic_slice_in_dim(line, (LINE - 1 - z) * rows, LINE * rows, 0)
    line = line.reshape(LINE, rows, columns)
    return line, lax.ppermute(line, "dp", OTHER_SIDE)


def gather_end(lines):
    if lax.axis_size("dp") != LINE * SIDE * CORE:
        return lines[0]
    _, x, c = place_of()
    pair = paired(*lines, x, 1)
    full = paired(pair, lax.ppermute(pair, "dp", OTHER_CORE), c, 2)
    return full.reshape(-1, full.shape[-1])


def part_of(blocks, at, axis):
    return lax.dynamic_index_in_dim(blocks, at, axis, keepdims=False)


def added(kept, got):
    return (kept.astype(f32) + got.astype(f32)).astype(bf16)


def scatter_start(values):
    if lax.axis_size("dp") != LINE * SIDE * CORE:
        return values
    c = place_of()[2]
    blocks = values.reshape(LINE, SIDE, CORE, -1, values.shape[1])
    got = lax.ppermute(part_of(blocks, 1 - c, 2), "dp", OTHER_CORE)
    return added(part_of(blocks, c, 2), got)


def scatter_middle(*blocks):
    if lax.axis_size("dp") != LINE * SIDE * CORE:
        return jnp.concatenate(blocks, axis=1), None
    x = place_of()[1]
    sent = jnp.concatenate([part_of(b, 1 - x, 1) for b in blocks], axis=-1)
    kept = jnp.concatenate([part_of(b, x, 1) for b in blocks], axis=-1)
    return kept, lax.ppermute(sent, "dp", OTHER_SIDE)


def scatter_added(kept, got, *earlier):
    return kept if got is None else added(kept, after(got, *earlier))


def scatter_end(blocks):
    if lax.axis_size("dp") != LINE * SIDE * CORE:
        return scatter_plain(blocks)
    return lax.psum_scatter(
        blocks.reshape(-1, blocks.shape[-1]), "dp", scatter_dimension=0, tiled=True,
        axis_index_groups=LINES,
    )


def after(values, *earlier):
    return lax.optimization_barrier((values, *earlier))[0]


def gather_plain(shard):
    return lax.all_gather(shard, "dp", axis=0, tiled=True)


def scatter_plain(values):
    return lax.psum_scatter(values, "dp", scatter_dimension=0, tiled=True)


def rolled(values):
    half = values.shape[0] // 2
    return jnp.concatenate([values[half:], values[:half]], axis=0)


def pad_lanes(values):
    return jnp.pad(values, ((0, 0), (0, LANES - values.shape[1])))


def local(
    residual_in, cotangent, input_gain, z_weight, x_weight, bc_weight, dt_weight,
    conv_inner, conv_inner_bias, conv_state, conv_state_bias, dt_bias, decay_log,
    skip_gain, gated_gain, out_weight,
):
    layers = input_gain.shape[0]
    half, width = residual_in.shape
    inner = gated_gain.shape[1]
    heads = dt_bias.shape[1]
    inner_total = inner * lax.axis_size("tensor")
    blocks = 2 * half // CHUNK
    bc_rows = bc_weight.shape[1]
    mine = lax.axis_index("tensor")
    rot = (mine * (blocks // 2)).astype(jnp.int32).reshape(1)

    bc_other = swap(bc_weight)
    bc_pair = jnp.where(
        mine == 0,
        jnp.concatenate([bc_weight, bc_other], axis=1),
        jnp.concatenate([bc_other, bc_weight], axis=1),
    )

    def first_shard(l):
        return jnp.concatenate([x_weight[l], bc_pair[l], pad_lanes(dt_weight[l])], axis=1)

    def project(rows, l):
        if l == 0:
            lines, w_first, w_out = weights[0]
            first = dot_nn(rows, w_first)
            w_z = gather_end((*lines[:-1], after(lines[-1], first)))
            weights[0] = (w_z, w_first, w_out)
            return dot_nn(rows, w_z), first, 0
        both = dot_nn(rows, weights[l][0])
        return both, both, inner

    weights = [(gather_start(z_weight[0]), gather_plain(first_shard(0)), gather_plain(out_weight[0].T))]
    for l in range(1, layers):
        both = jnp.concatenate([z_weight[l], first_shard(l)], axis=1)
        weights.append((gather_plain(both), gather_plain(out_weight[l].T)))

    def params_of(l):
        rate = pad_lanes(-jnp.exp(decay_log[l])[None])
        return (
            conv_inner[l], conv_inner_bias[l][None], conv_state[l], conv_state_bias[l][None],
            rate, jnp.repeat(skip_gain[l], HEADDIM)[None], gated_gain[l][None],
        )

    saved = []
    hidden = residual_in
    for l in range(layers):
        w_out = weights[l][-1]
        scale = lax.rsqrt(jnp.mean(hidden * hidden, axis=1, keepdims=True) + epsilon)
        normed = (hidden * scale * input_gain[l]).astype(bf16)
        rows = jnp.concatenate([normed, swap(normed)], axis=0)
        zs, first, first_at = project(rows, l)
        raw_step = first[:, first_at + inner + 2 * LANES :] + pad_lanes(dt_bias[l][None])
        step = jax.nn.softplus(raw_step)
        sig = jax.nn.sigmoid(raw_step)
        params = params_of(l)
        ghat, squares, y, *kept = scan_forward(rot, zs, first, first_at, step, *params)
        squares = squares + rolled(swap(squares))
        q = lax.rsqrt(squares / inner_total + epsilon)
        q_col = q.reshape(2 * half, 1)
        if l == layers - 1:
            out = dot_nt(ghat, w_out) * q_col
            flow_low = cotangent.astype(bf16)
            go = jnp.concatenate([flow_low, swap(flow_low)], axis=0)
            part = jnp.sum(go.astype(f32) * out, axis=1).reshape(blocks, 1, CHUNK)
            other = swap(part)
            dots = part + rolled(other)
            out_sent = after(out[half:].astype(bf16), other)
            branch_got = swap(out_sent)
            branch = out[:half] + branch_got.astype(f32)
        else:
            dots = None
            out_sent = (dot_nt(ghat[half:], w_out) * q_col[half:]).astype(bf16)
            ghat, out_sent = lax.optimization_barrier((ghat, out_sent))
            out_own = dot_nt(ghat[:half], w_out) * q_col[:half]
            out_own, out_got = lax.optimization_barrier((out_own, swap(out_sent)))
            branch = out_own + out_got.astype(f32)
        saved.append((hidden, scale, rows, zs, first, first_at, step, sig, params, ghat, y, kept, q, q_col, branch))
        hidden = hidden + branch

    flow = cotangent
    summed = []
    large, early, late = [None] * layers, [None] * layers, [None] * layers
    for l in reversed(range(layers)):
        w_out = weights[l][-1]
        (
            hidden_in, scale, rows, zs, first, first_at, step, sig, params, ghat, y, kept, q, q_col,
            branch,
        ) = saved[l]
        if l < layers - 1:
            flow_low = flow.astype(bf16)
            part = jnp.sum(flow_low.astype(f32) * branch, axis=1).reshape(blocks // 2, 1, CHUNK)
            dots = jnp.concatenate([part, swap(part)], axis=0)
            go = jnp.concatenate([flow_low, swap(flow_low)], axis=0)
        qc = q * q * dots / inner_total
        go_scaled = (go.astype(f32) * q_col).astype(bf16)
        if l == 0:
            g_out = dot_tn(go_scaled, ghat).astype(bf16)
            go, g_out = lax.optimization_barrier((go, g_out))
            g_out = scatter_start(g_out)
            d_yn = dot_nn(go, w_out)
            z_sig = jax.nn.sigmoid(zs)
            d_gated = d_yn * params[-1] * q_col - y * (zs * z_sig) * qc.reshape(2 * half, 1)
            dz = (d_gated * y * (z_sig * (1.0 + zs * (1.0 - z_sig)))).astype(bf16)
            dz, g_out = lax.optimization_barrier((dz, g_out))
            g_z = dot_tn(rows, dz).astype(bf16)
            dz, g_z = lax.optimization_barrier((dz, g_z))
            g_z = scatter_start(g_z)
            d_rows = dot_nt(dz, weights[0][0])
            d_yn, g_out, g_z, d_rows = lax.optimization_barrier((d_yn, g_out, g_z, d_rows))
            g_pair = scatter_middle(g_out, g_z)
        else:
            d_yn = dot_nn(go, w_out)
            g_out = dot_tn(go_scaled, ghat).astype(bf16)
            d_yn, g_out = lax.optimization_barrier((d_yn, g_out))
            g_out = scatter_plain(g_out)
        d_proj, gx, gs, gh = scan_backward(
            rot, l > 0, zs, first, first_at, step, sig, y, *kept, d_yn, q, qc, *params
        )
        if l == 0:
            g_first = dot_tn(rows, after(d_proj, *summed)).astype(bf16)
            d_proj, g_first = lax.optimization_barrier((d_proj, g_first))
            g_pair = scatter_added(*g_pair, g_first)
            g_first = scatter_start(g_first)
            d_proj = after(d_proj, g_pair)
            d_sent = (dot_nt(d_proj[half:], weights[0][1]) + d_rows[half:]).astype(bf16)
            d_proj, d_sent = lax.optimization_barrier((d_proj, d_sent))
            d_own = dot_nt(d_proj[:half], weights[0][1]) + d_rows[:half]
        else:
            d_sent = dot_nt(d_proj[half:], weights[l][0]).astype(bf16)
            d_proj, d_sent = lax.optimization_barrier((d_proj, d_sent))
            d_own = dot_nt(d_proj[:half], weights[l][0])
        if l == layers - 1:
            d_sent = after(d_sent, branch_got)
        d_got = swap(d_sent)
        if l == 0:
            g_pair = scatter_end(g_pair)
            g_first = scatter_added(*scatter_middle(after(g_first, d_sent)))
            d_got = after(d_got, g_first, g_pair)
            g_first, g_pair = scatter_end(g_first).astype(f32), after(g_pair, d_got).astype(f32)
            g_out, g_z = g_pair[:, :inner], g_pair[:, inner:]
        else:
            g_all = dot_tn(rows, after(d_proj, d_sent)).astype(bf16)
            d_got, g_all = lax.optimization_barrier((d_got, g_all))
            g_all = scatter_plain(after(g_all, g_out))
            summed.append(g_all)
            g_all = g_all.astype(f32)
            g_z, g_first, g_out = g_all[:, :inner], g_all[:, inner:], g_out.astype(f32)
        d_own, d_got = lax.optimization_barrier((d_own, d_got))
        d_normed = d_own + d_got.astype(f32)
        g_bc = g_first[:, inner : inner + 2 * LANES]
        bc_sent = lax.dynamic_slice_in_dim(g_bc, (1 - mine) * bc_rows, bc_rows, 0)
        g_bc = lax.dynamic_slice_in_dim(g_bc, mine * bc_rows, bc_rows, 0) + swap(bc_sent)

        weighted = d_normed * input_gain[l]
        g_gain = jnp.sum(d_normed * hidden_in * scale, axis=0).reshape(-1, LANES)
        inner_dot = jnp.sum(weighted * hidden_in, axis=1, keepdims=True)
        flow = flow + scale * weighted - hidden_in * (scale * scale * scale * inner_dot / width)
        large[l] = (
            g_z, g_first[:, :inner], g_bc,
            g_first[:, inner + 2 * LANES : inner + 2 * LANES + heads], g_out.T,
        )
        early[l] = (gs[:5].reshape(-1, LANES), gx[:7].reshape(-1, LANES), gh[:2])
        late[l] = g_gain

    shared = jnp.concatenate([e[0] for e in early] + late, axis=0)
    shared = shared + swap(shared)
    small = butterfly(jnp.concatenate([shared] + [part for e in early for part in e[1:]], axis=0))
    at = 0

    def take(*shape):
        nonlocal at
        size = 1
        for s in shape:
            size *= s
        at += size // LANES
        return small[at - size // LANES : at].reshape(shape)

    r_state = jnp.stack([take(5, 2 * LANES) for _ in range(layers)])
    r_gain = jnp.stack([take(width) for _ in range(layers)])
    r_inner, r_head = zip(*[(take(7, inner), take(2, LANES)) for _ in range(layers)])
    r_inner, r_head = jnp.stack(r_inner), jnp.stack(r_head)[:, :, :heads]
    g_z, g_x, g_bc, g_dt, g_out = (jnp.stack(parts) for parts in zip(*large))
    return (
        hidden, flow, r_gain, g_z, g_x, g_bc, g_dt,
        r_inner[:, :4], r_inner[:, 4], r_state[:, :4], r_state[:, 4],
        r_head[:, 0], r_head[:, 1],
        jnp.sum(r_inner[:, 5].reshape(layers, heads, HEADDIM), axis=2), r_inner[:, 6], g_out,
    )


def solution(mesh):
    row = P(("dp", "tensor"), None)
    rest = (
        P(), P(None, "dp", "tensor"), P(None, "dp", "tensor"), P(None, ("dp", "tensor"), None),
        P(None, "dp", "tensor"), P(None, None, "tensor"), P(None, "tensor"), P(), P(),
        P(None, "tensor"), P(None, "tensor"), P(None, "tensor"), P(None, "tensor"),
        P(None, "tensor", "dp"),
    )
    specs = (row, row, *rest)
    return jax.shard_map(local, mesh=mesh, in_specs=specs, out_specs=specs, check_vma=False)
```

```python
import functools

import jax
import jax.numpy as jnp
from jax import lax
from jax.experimental import pallas as pl
from jax.experimental.pallas import tpu as pltpu
from jax.sharding import PartitionSpec as P

HEADDIM = 64
CHUNK = 128
LANES = 128
WIDE = 256
epsilon = 1e-05
f32 = jnp.float32
bf16 = jnp.bfloat16


def dot_nn(left, right):
    return lax.dot_general(left, right, (((1,), (0,)), ((), ())), preferred_element_type=f32)


def dot_nt(left, right):
    return lax.dot_general(left, right, (((1,), (1,)), ((), ())), preferred_element_type=f32)


def dot_tn(left, right):
    return lax.dot_general(left, right, (((0,), (0,)), ((), ())), preferred_element_type=f32)


def conv_rows(ext, kernel, offset, length):
    total = offset + kernel[0:1] * ext[5 : 5 + length]
    for tap in range(1, 4):
        total = total + kernel[tap : tap + 1] * ext[5 + tap : 5 + tap + length]
    return total


def row_col(size):
    return (
        lax.broadcasted_iota(jnp.int32, (size, size), 0),
        lax.broadcasted_iota(jnp.int32, (size, size), 1),
    )


def decays(dt_ref, rate_ref, lower):
    step = dt_ref[...]
    lower = lower.astype(bf16)
    cum = dot_nn(jnp.concatenate([lower] * 3, axis=1), three_parts(step * rate_ref[...]))
    last = cum[CHUNK - 1 : CHUNK]
    return step, cum, cum.T, last, jnp.exp(cum), jnp.exp(last - cum)


def two_parts(values, axis):
    high = values.astype(bf16)
    return jnp.concatenate([high, (values - high.astype(f32)).astype(bf16)], axis=axis)


def three_parts(values):
    high = values.astype(bf16)
    rest = values - high.astype(f32)
    middle = rest.astype(bf16)
    return jnp.concatenate([high, middle, (rest - middle.astype(f32)).astype(bf16)], axis=0)


def heads_of(channels, axis):
    shape = (channels, LANES) if axis == 0 else (LANES, channels)
    at = lax.broadcasted_iota(jnp.int32, shape, axis)
    head = lax.broadcasted_iota(jnp.int32, shape, 1 - axis)
    return jnp.where((at >= head * HEADDIM) & (at < (head + 1) * HEADDIM), 1.0, 0.0).astype(bf16)


def block_diagonal(values, low_half):
    zero = jnp.zeros_like(values)
    return jnp.concatenate(
        [jnp.where(low_half, values, zero), jnp.where(low_half, zero, values)], axis=0
    )


def forward_kernel(
    rot_ref, xr_ref, bcr_ref, dt_ref, zr_ref,
    cw_ref, cb_ref, sw_ref, sb_ref, rate_ref, skip_ref, gain_ref,
    ghat_ref, ssq_ref, y_ref, s_ref, pre_ref, bc_pre_ref,
    state, x_halo, bc_halo, widen, wide,
):
    @pl.when(pl.program_id(0) == 0)
    def _():
        widen[...] = jnp.concatenate([heads_of(xr_ref.shape[1], 1)] * 2, axis=0)
        state[...] = jnp.zeros_like(state)
        x_halo[...] = jnp.zeros_like(x_halo)
        bc_halo[...] = jnp.zeros_like(bc_halo)

    rows, cols = row_col(CHUNK)
    causal = rows >= cols
    low_half = cols < HEADDIM
    step, cum, cum_t, last, grow, tail = decays(dt_ref, rate_ref, jnp.where(causal, 1.0, 0.0))
    wide[...] = dot_nn(two_parts(jnp.concatenate([step, grow, tail], axis=0), 1), widen[...])
    last_grow = jnp.exp(last)
    bc_ext = jnp.concatenate([bc_halo[...], bcr_ref[...]], axis=0)
    bc_halo[...] = bcr_ref[CHUNK - 8 :]
    bc_pre = conv_rows(bc_ext, sw_ref[...], sb_ref[...], CHUNK)
    bc_pre_ref[...] = bc_pre
    bc = (bc_pre * jax.nn.sigmoid(bc_pre)).astype(bf16)
    b_low, c_low = bc[:, :LANES], bc[:, LANES:]
    b_turned = b_low.astype(f32).T.astype(bf16)
    mix = jnp.where(causal, dot_nt(c_low, b_low), 0.0)
    squares = jnp.zeros((CHUNK, LANES), f32)

    def spread(cols_of, quad):
        low = low_half[: cols_of.shape[0]]
        return jnp.concatenate(
            [
                jnp.where(low, cols_of[:, h : h + 1], cols_of[:, h + 1 : h + 2])
                for h in (4 * quad, 4 * quad + 2)
            ],
            axis=1,
        )

    for quad in range(xr_ref.shape[1] // WIDE):
        at = slice(quad * WIDE, (quad + 1) * WIDE)
        xr = xr_ref[:, at]
        ext = jnp.concatenate([x_halo[:, at], xr], axis=0)
        x_halo[:, at] = xr[CHUNK - 8 :]
        pre = conv_rows(ext, cw_ref[:, at], cb_ref[:, at], CHUNK)
        pre_ref[:, at] = pre
        x = (pre * jax.nn.sigmoid(pre)).astype(bf16).astype(f32)
        x_stepped = x * wide[:CHUNK, at]
        x_step = x_stepped.astype(bf16)
        s_in = state[:, at]
        s_low = s_in.astype(bf16)
        s_ref[0, :, at] = s_low
        parts = []
        for pair in range(2):
            mixed = []
            for h in range(4 * quad + 2 * pair, 4 * quad + 2 * pair + 2):
                decay = jnp.exp(jnp.minimum(cum[:, h : h + 1] - cum_t[h : h + 1, :], 0.0))
                mixed.append((mix * decay).astype(bf16))
            right = block_diagonal(x_step[:, pair * LANES : (pair + 1) * LANES], low_half)
            parts.append(dot_nn(jnp.concatenate(mixed, axis=1), right))
        across = dot_nn(c_low, s_low) * wide[CHUNK : 2 * CHUNK, at]
        y = jnp.concatenate(parts, axis=1) + across + skip_ref[:, at] * x
        y_ref[:, at] = y
        z = zr_ref[:, at]
        gated = y * (z * jax.nn.sigmoid(z))
        squared = gated * gated
        squares = squares + (squared[:, :LANES] + squared[:, LANES:])
        ghat_ref[:, at] = (gated * gain_ref[:, at]).astype(bf16)
        fresh = dot_nn(b_turned, (x_stepped * wide[2 * CHUNK :, at]).astype(bf16))
        state[:, at] = s_in * spread(last_grow, quad) + fresh
    ssq_ref[0] = jnp.sum(squares.T, axis=0, keepdims=True)


def backward_kernel(
    gate_at, x_at, rot_ref, xr_ref, pre_ref, bcr_ref, bc_pre_ref, dt_ref, sig_ref, zr_ref, y_ref, s_ref, dyn_ref, q_ref, qc_ref,
    cw_ref, sw_ref, rate_ref, skip_ref, gain_ref,
    dp_ref, gx_ref, gs_ref, gh_ref,
    dstate, x_halo, bc_halo, narrow, products, crossings, gx_parts, gs_parts, gh_parts,
):
    inner = xr_ref.shape[1]
    first = pl.program_id(0) == pl.num_programs(0) - 1

    @pl.when(pl.program_id(0) == 0)
    def _():
        dstate[...] = jnp.zeros_like(dstate)
        x_halo[...] = jnp.zeros_like(x_halo)
        bc_halo[...] = jnp.zeros_like(bc_halo)
        narrow[...] = heads_of(inner, 0)
        gx_parts[...] = jnp.zeros_like(gx_parts)
        gs_parts[...] = jnp.zeros_like(gs_parts)
        gh_parts[...] = jnp.zeros_like(gh_parts)

    rows, cols = row_col(CHUNK)
    upper = cols >= rows
    low_half = cols < HEADDIM
    step, cum, cum_t, last, grow, tail = decays(dt_ref, rate_ref, jnp.where(rows >= cols, 1.0, 0.0))
    last_grow = jnp.exp(last)
    bcr = bcr_ref[...]
    bc_pre = bc_pre_ref[...]
    bc_sig = jax.nn.sigmoid(bc_pre)
    bc = (bc_pre * bc_sig).astype(bf16)
    b_low, c_low = bc[:, :LANES], bc[:, LANES:]
    c_turned = c_low.astype(f32).T.astype(bf16)
    mix = jnp.where(upper, dot_nt(b_low, c_low), 0.0)
    q = jnp.broadcast_to(q_ref[0], (WIDE, CHUNK)).T
    qc = jnp.broadcast_to(qc_ref[0], (WIDE, CHUNK)).T

    def spread(cols_of, quad):
        low = low_half[: cols_of.shape[0]]
        return jnp.concatenate(
            [
                jnp.where(low, cols_of[:, h : h + 1], cols_of[:, h + 1 : h + 2])
                for h in (4 * quad, 4 * quad + 2)
            ],
            axis=1,
        )

    def add_to(parts, index, at, values):
        parts[8 * index : 8 * index + 8, at] += jnp.sum(
            values.reshape(CHUNK // 8, 8, values.shape[1]), axis=0
        )

    d_mix = jnp.zeros((CHUNK, CHUNK), f32)
    d_b = jnp.zeros((CHUNK, LANES), f32)
    d_c = jnp.zeros((CHUNK, LANES), f32)
    for quad in range(inner // WIDE):
        at = slice(quad * WIDE, (quad + 1) * WIDE)
        xr = xr_ref[:, at]
        pre = pre_ref[:, at]
        sig = jax.nn.sigmoid(pre)
        x_low = (pre * sig).astype(bf16)
        x = x_low.astype(f32)
        step_wide = spread(step, quad)
        x_stepped = x * step_wide
        x_step = x_stepped.astype(bf16)
        z = zr_ref[:, at]
        z_sig = jax.nn.sigmoid(z)
        z_act = z * z_sig
        y = y_ref[:, at]
        gated = y * z_act
        dyn = dyn_ref[:, at]
        add_to(gx_parts, 6, at, dyn * gated * q)
        d_gated = dyn * (gain_ref[:, at] * q) - gated * qc
        if gate_at is not None:
            dp_ref[:, at] = (d_gated * y * (z_sig * (1.0 + z * (1.0 - z_sig)))).astype(bf16)
        dy = d_gated * z_act
        dy_low = dy.astype(bf16)
        dy_wide = dy_low.astype(f32)
        add_to(gx_parts, 5, at, dy * x)
        ds = dstate[:, at]
        ds_low = ds.astype(bf16)
        parts = []
        for pair in range(2):
            half = slice(pair * LANES, (pair + 1) * LANES)
            own = [
                jnp.exp(jnp.minimum(cum_t[h : h + 1, :] - cum[:, h : h + 1], 0.0))
                for h in range(4 * quad + 2 * pair, 4 * quad + 2 * pair + 2)
            ]
            right = block_diagonal(dy_low[:, half], low_half)
            mixed = jnp.concatenate([(mix * decay).astype(bf16) for decay in own], axis=1)
            parts.append(dot_nn(mixed, right))
            d_mixed = dot_nt(x_step[:, half], right)
            d_mix = d_mix + d_mixed[:, :CHUNK] * own[0] + d_mixed[:, CHUNK:] * own[1]
        within = jnp.concatenate(parts, axis=1)
        tail_wide = spread(tail, quad)
        beyond = dot_nn(b_low, ds_low) * tail_wide
        skip = skip_ref[:, at]
        dx = step_wide * (within + beyond) + skip * dy
        moved = dy_wide * (y - skip * x) - x_step.astype(f32) * within
        products[: 2 * CHUNK, at] = two_parts(moved, 0)
        products[2 * CHUNK : 3 * CHUNK, at] = (x * within).astype(bf16)
        products[3 * CHUNK :, at] = (x * beyond).astype(bf16)
        s_low = s_ref[0, :, at]
        crossings[:, at] = jnp.sum(
            (ds * s_low.astype(f32)).reshape(CHUNK // 8, 8, WIDE), axis=0
        )
        dy_grow = (dy_wide * spread(grow, quad)).astype(bf16)
        d_c = d_c + dot_nt(dy_grow, s_low)
        d_b = d_b + dot_nt((x_stepped * tail_wide).astype(bf16), ds_low)
        dstate[:, at] = ds * spread(last_grow, quad) + dot_nn(c_turned, dy_grow)
        d_pre = dx * (sig * (1.0 + pre * (1.0 - sig)))
        d_ext = jnp.concatenate([d_pre, x_halo[:, at]], axis=0)
        x_halo[:, at] = d_pre[:8]
        d_raw = cw_ref[3:4, at] * d_pre
        for tap in range(3):
            moved = d_ext[3 - tap : 3 - tap + CHUNK]
            d_raw = d_raw + cw_ref[tap : tap + 1, at] * moved
            add_to(gx_parts, tap, at, moved * xr)
        add_to(gx_parts, 3, at, d_pre * xr)
        add_to(gx_parts, 4, at, d_pre)
        dp_ref[:, x_at + at.start : x_at + at.stop] = d_raw.astype(bf16)
    d_mix = jnp.where(upper, d_mix, 0.0)
    d_b = d_b + dot_nn(d_mix.astype(bf16), c_low)
    d_c = d_c + dot_nn(d_mix.T.astype(bf16), b_low)
    d_bc = jnp.concatenate([d_b, d_c], axis=1)
    d_pre = d_bc * (bc_sig * (1.0 + bc_pre * (1.0 - bc_sig)))
    d_ext = jnp.concatenate([d_pre, bc_halo[...]], axis=0)
    bc_halo[...] = d_pre[:8]
    d_raw = sw_ref[3:4] * d_pre
    whole = slice(None)
    for tap in range(3):
        moved = d_ext[3 - tap : 3 - tap + CHUNK]
        d_raw = d_raw + sw_ref[tap : tap + 1] * moved
        add_to(gs_parts, tap, whole, moved * bcr)
    add_to(gs_parts, 3, whole, d_pre * bcr)
    add_to(gs_parts, 4, whole, d_pre)
    dp_ref[:, x_at + inner : x_at + inner + 2 * LANES] = d_raw.astype(bf16)
    sums = dot_nn(products[...], narrow[...])
    d_cum = sums[:CHUNK] + sums[CHUNK : 2 * CHUNK]
    d_beyond = sums[3 * CHUNK :]
    through = jnp.sum(dot_nn(two_parts(crossings[...], 0), narrow[...]), axis=0, keepdims=True)
    later = jnp.where(upper, 1.0, 0.0).astype(bf16)
    d_log = through * last_grow + dot_nn(
        jnp.concatenate([later] * 3 + [1 - later] * 3, axis=1),
        jnp.concatenate([three_parts(d_cum), three_parts(step * d_beyond)], axis=0),
    )
    rate = rate_ref[...]
    d_raw_step = (d_log * rate + sums[2 * CHUNK : 3 * CHUNK] + d_beyond) * sig_ref[...]
    add_to(gh_parts, 0, whole, d_raw_step)
    add_to(gh_parts, 1, whole, d_log * step * rate)
    dp_ref[:, x_at + inner + 2 * LANES :] = d_raw_step.astype(bf16)

    @pl.when(first)
    def _():
        for parts, ref in ((gx_parts, gx_ref), (gs_parts, gs_ref), (gh_parts, gh_ref)):
            width = ref.shape[1]
            ref[...] = jnp.sum(parts[...].reshape(8, 8, width), axis=1)


def in_hbm(*arrays):
    return [pltpu.with_memory_space_constraint(array, pltpu.HBM) for array in arrays]


def whole_spec(array):
    return pl.BlockSpec(array.shape, lambda c, rot: (0,) * array.ndim)


def rows_kernel(rows_ref, weight_ref, *refs):
    refs[-1][...] = dot_nn(rows_ref[...], weight_ref[...])


def rows_product(rows, weight, tile, into=None):
    height, depth = rows.shape
    columns = weight.shape[1]
    place = 0 if into is None else 1
    specs = [
        pl.BlockSpec((height, depth), lambda j: (0, 0)),
        pl.BlockSpec((depth, tile), lambda j: (0, j)),
    ]
    rest = () if into is None else (into,)
    return pl.pallas_call(
        rows_kernel,
        grid=(columns // tile,),
        in_specs=specs + [pl.BlockSpec(memory_space=pl.ANY)] * len(rest),
        out_specs=pl.BlockSpec((height, tile), lambda j: (place, j)),
        out_shape=pltpu.HBM((2 * height, columns), f32),
        input_output_aliases={2: 0} if rest else {},
        compiler_params=pltpu.CompilerParams(
            dimension_semantics=("arbitrary",), vmem_limit_bytes=24 * 2**20
        ),
        cost_estimate=pl.CostEstimate(
            flops=2 * height * depth * columns,
            bytes_accessed=2 * depth * columns + 4 * height * columns,
            transcendentals=0,
        ),
        name="rows_product",
    )(rows, *in_hbm(weight), *rest)


def scan_forward(rot, zs, first, first_at, step, conv, conv_bias, conv_s, conv_s_bias, rate, skip, gain):
    length, inner = zs.shape[0], gain.shape[1]
    blocks = length // CHUNK

    def place(width, column=0):
        return pl.BlockSpec((CHUNK, width), lambda c, rot: ((c + rot[0]) % blocks, column))

    params = (conv, conv_bias, conv_s, conv_s_bias, rate, skip, gain)
    return pl.pallas_call(
        forward_kernel,
        grid_spec=pltpu.PrefetchScalarGridSpec(
            num_scalar_prefetch=1,
            grid=(blocks,),
            in_specs=[
                place(inner, first_at // inner), place(2 * LANES, (first_at + inner) // (2 * LANES)), place(LANES), place(inner),
                *map(whole_spec, params),
            ],
            out_specs=[
                place(inner),
                pl.BlockSpec((1, 1, CHUNK), lambda c, rot: ((c + rot[0]) % blocks, 0, 0)),
                place(inner),
                pl.BlockSpec((1, LANES, inner), lambda c, rot: (c, 0, 0)),
                place(inner), place(2 * LANES),
            ],
            scratch_shapes=[
                pltpu.VMEM((LANES, inner), f32),
                pltpu.VMEM((8, inner), f32),
                pltpu.VMEM((8, 2 * LANES), f32),
                pltpu.VMEM((2 * LANES, inner), bf16),
                pltpu.VMEM((3 * CHUNK, inner), f32),
            ],
        ),
        out_shape=[
            jax.ShapeDtypeStruct((length, inner), bf16),
            jax.ShapeDtypeStruct((blocks, 1, CHUNK), f32),
            pltpu.HBM((length, inner), f32),
            pltpu.HBM((blocks, LANES, inner), bf16),
            pltpu.HBM((length, inner), f32),
            pltpu.HBM((length, 2 * LANES), f32),
        ],
        compiler_params=pltpu.CompilerParams(
            dimension_semantics=("arbitrary",), vmem_limit_bytes=20 * 2**20
        ),
        cost_estimate=pl.CostEstimate(
            flops=int(25e9), bytes_accessed=25 * 2**20, transcendentals=0
        ),
        name="scan_forward",
    )(rot, *in_hbm(first, first), step, *in_hbm(zs), *params)


def scan_backward(
    rot, with_gate, zs, first, first_at, step, sig, y, states, pre, bc_pre, d_yn, q, qc,
    conv, conv_bias, conv_s, conv_s_bias, rate, skip, gain,
):
    length, inner = zs.shape[0], gain.shape[1]
    blocks = length // CHUNK

    def place(width, column=0):
        return pl.BlockSpec(
            (CHUNK, width), lambda c, rot: ((blocks - 1 - c + rot[0]) % blocks, column)
        )

    def fixed(height, width):
        return pl.BlockSpec((height, width), lambda c, rot: (0, 0))

    line = pl.BlockSpec(
        (1, 1, CHUNK), lambda c, rot: ((blocks - 1 - c + rot[0]) % blocks, 0, 0)
    )
    params = (conv, conv_s, rate, skip, gain)
    x_at, bc_at = first_at // inner, (first_at + inner) // (2 * LANES)
    out_width = (2 if with_gate else 1) * inner + 3 * LANES
    kernel = functools.partial(
        backward_kernel, 0 if with_gate else None, inner if with_gate else 0
    )
    return pl.pallas_call(
        kernel,
        grid_spec=pltpu.PrefetchScalarGridSpec(
            num_scalar_prefetch=1,
            grid=(blocks,),
            in_specs=[
                place(inner, x_at), place(inner), place(2 * LANES, bc_at), place(2 * LANES),
                place(LANES), place(LANES), place(inner), place(inner),
                pl.BlockSpec((1, LANES, inner), lambda c, rot: (blocks - 1 - c, 0, 0)),
                place(inner), line, line,
                *map(whole_spec, params),
            ],
            out_specs=[
                place(out_width),
                fixed(8, inner), fixed(8, 2 * LANES), fixed(8, LANES),
            ],
            scratch_shapes=[
                pltpu.VMEM((LANES, inner), f32),
                pltpu.VMEM((8, inner), f32),
                pltpu.VMEM((8, 2 * LANES), f32),
                pltpu.VMEM((inner, LANES), bf16),
                pltpu.VMEM((4 * CHUNK, inner), bf16),
                pltpu.VMEM((8, inner), f32),
                pltpu.VMEM((64, inner), f32),
                pltpu.VMEM((64, 2 * LANES), f32),
                pltpu.VMEM((64, LANES), f32),
            ],
        ),
        out_shape=[
            jax.ShapeDtypeStruct((length, out_width), bf16),
            jax.ShapeDtypeStruct((8, inner), f32),
            jax.ShapeDtypeStruct((8, 2 * LANES), f32),
            jax.ShapeDtypeStruct((8, LANES), f32),
        ],
        compiler_params=pltpu.CompilerParams(
            dimension_semantics=("arbitrary",), vmem_limit_bytes=28 * 2**20
        ),
        cost_estimate=pl.CostEstimate(
            flops=int(10e9), bytes_accessed=40 * 2**20, transcendentals=0
        ),
        name="scan_backward",
    )(rot, *in_hbm(first, pre, first, bc_pre), step, sig, *in_hbm(zs, y, states, d_yn), q, qc, *params)


TENSOR_SWAP = [(0, 1), (1, 0)]


def swap(values):
    return lax.ppermute(values, "tensor", TENSOR_SWAP)


def butterfly(values):
    size = lax.axis_size("dp")
    step = 1
    while step < size:
        values = values + lax.ppermute(values, "dp", [(i, i ^ step) for i in range(size)])
        step *= 2
    return values


LINE, SIDE, CORE = 4, 2, 2
PLACES = [(z, x, c) for z in range(LINE) for x in range(SIDE) for c in range(CORE)]


def index_of(z, x, c):
    return (z * SIDE + x) * CORE + c


def along_line(step, lowest, highest_place):
    return [
        (index_of(z, x, c), index_of(z + step, x, c))
        for z, x, c in PLACES
        if lowest <= z <= highest_place
    ]


OTHER_SIDE = [(index_of(z, x, c), index_of(z, 1 - x, c)) for z, x, c in PLACES]
OTHER_CORE = [(index_of(z, x, c), index_of(z, x, 1 - c)) for z, x, c in PLACES]
LINES = [[index_of(z, x, c) for z in range(LINE)] for x in range(SIDE) for c in range(CORE)]


def place_of():
    at = lax.axis_index("dp")
    return at // (SIDE * CORE), (at // CORE) % SIDE, at % CORE


def paired(own, other, mine, axis):
    return jnp.where(
        mine == 0, jnp.stack([own, other], axis=axis), jnp.stack([other, own], axis=axis)
    )


def gather_start(shard):
    if lax.axis_size("dp") != LINE * SIDE * CORE:
        return (lax.all_gather(shard, "dp", axis=0, tiled=True),)
    z = place_of()[0]
    rows, columns = shard.shape
    right, left = [shard], [shard]
    for step in range(1, LINE):
        right.append(lax.ppermute(right[-1], "dp", along_line(1, step - 1, LINE - 2)))
        left.append(lax.ppermute(left[-1], "dp", along_line(-1, 1, LINE - step)))
    line = jnp.concatenate(right[:0:-1] + left, axis=0)
    line = lax.dynamic_slice_in_dim(line, (LINE - 1 - z) * rows, LINE * rows, 0)
    line = line.reshape(LINE, rows, columns)
    return line, lax.ppermute(line, "dp", OTHER_SIDE)


def gather_end(lines):
    if lax.axis_size("dp") != LINE * SIDE * CORE:
        return lines[0]
    _, x, c = place_of()
    pair = paired(*lines, x, 1)
    full = paired(pair, lax.ppermute(pair, "dp", OTHER_CORE), c, 2)
    return full.reshape(-1, full.shape[-1])


def part_of(blocks, at, axis):
    return lax.dynamic_index_in_dim(blocks, at, axis, keepdims=False)


def added(kept, got):
    return (kept.astype(f32) + got.astype(f32)).astype(bf16)


def scatter_start(values):
    if lax.axis_size("dp") != LINE * SIDE * CORE:
        return values
    c = place_of()[2]
    blocks = values.reshape(LINE, SIDE, CORE, -1, values.shape[1])
    got = lax.ppermute(part_of(blocks, 1 - c, 2), "dp", OTHER_CORE)
    return added(part_of(blocks, c, 2), got)


def scatter_middle(*blocks):
    if lax.axis_size("dp") != LINE * SIDE * CORE:
        return jnp.concatenate(blocks, axis=1), None
    x = place_of()[1]
    sent = jnp.concatenate([part_of(b, 1 - x, 1) for b in blocks], axis=-1)
    kept = jnp.concatenate([part_of(b, x, 1) for b in blocks], axis=-1)
    return kept, lax.ppermute(sent, "dp", OTHER_SIDE)


def scatter_added(kept, got, *earlier):
    return kept if got is None else added(kept, after(got, *earlier))


def scatter_end(blocks):
    if lax.axis_size("dp") != LINE * SIDE * CORE:
        return scatter_plain(blocks)
    return lax.psum_scatter(
        blocks.reshape(-1, blocks.shape[-1]), "dp", scatter_dimension=0, tiled=True,
        axis_index_groups=LINES,
    )


def after(values, *earlier):
    return lax.optimization_barrier((values, *earlier))[0]


def gather_plain(shard):
    return lax.all_gather(shard, "dp", axis=0, tiled=True)


def scatter_plain(values):
    return lax.psum_scatter(values, "dp", scatter_dimension=0, tiled=True)


def rolled(values):
    half = values.shape[0] // 2
    return jnp.concatenate([values[half:], values[:half]], axis=0)


def pad_lanes(values):
    return jnp.pad(values, ((0, 0), (0, LANES - values.shape[1])))


def local(
    residual_in, cotangent, input_gain, z_weight, x_weight, bc_weight, dt_weight,
    conv_inner, conv_inner_bias, conv_state, conv_state_bias, dt_bias, decay_log,
    skip_gain, gated_gain, out_weight,
):
    layers = input_gain.shape[0]
    half, width = residual_in.shape
    inner = gated_gain.shape[1]
    heads = dt_bias.shape[1]
    inner_total = inner * lax.axis_size("tensor")
    blocks = 2 * half // CHUNK
    bc_rows = bc_weight.shape[1]
    mine = lax.axis_index("tensor")
    rot = (mine * (blocks // 2)).astype(jnp.int32).reshape(1)

    bc_other = swap(bc_weight)
    bc_pair = jnp.where(
        mine == 0,
        jnp.concatenate([bc_weight, bc_other], axis=1),
        jnp.concatenate([bc_other, bc_weight], axis=1),
    )

    def first_shard(l):
        return jnp.concatenate([x_weight[l], bc_pair[l], pad_lanes(dt_weight[l])], axis=1)

    def project(rows, l):
        if l == 0:
            lines, w_first, w_out = weights[0]
            rows = jnp.concatenate(rows, axis=0)
            first = dot_nn(rows, w_first)
            w_z = gather_end((*lines[:-1], after(lines[-1], first)))
            weights[0] = (w_z, w_first, w_out)
            return dot_nn(rows, w_z), first, 0
        both = rows_product(rows[0], weights[l][0], 9 * LANES)
        both = rows_product(rows[1], weights[l][0], 9 * LANES, both)
        return both, both, inner

    weights = [(gather_start(z_weight[0]), gather_plain(first_shard(0)), gather_plain(out_weight[0].T))]
    for l in range(1, layers):
        both = jnp.concatenate([z_weight[l], first_shard(l)], axis=1)
        weights.append((gather_plain(both), gather_plain(out_weight[l].T)))

    def params_of(l):
        rate = pad_lanes(-jnp.exp(decay_log[l])[None])
        return (
            conv_inner[l], conv_inner_bias[l][None], conv_state[l], conv_state_bias[l][None],
            rate, jnp.repeat(skip_gain[l], HEADDIM)[None], gated_gain[l][None],
        )

    saved = []
    hidden = residual_in
    for l in range(layers):
        w_out = weights[l][-1]
        scale = lax.rsqrt(jnp.mean(hidden * hidden, axis=1, keepdims=True) + epsilon)
        normed = (hidden * scale * input_gain[l]).astype(bf16)
        halves = (normed, swap(normed))
        zs, first, first_at = project(halves, l)
        rows = jnp.concatenate(halves, axis=0)
        raw_step = first[:, first_at + inner + 2 * LANES :] + pad_lanes(dt_bias[l][None])
        step = jax.nn.softplus(raw_step)
        sig = jax.nn.sigmoid(raw_step)
        params = params_of(l)
        ghat, squares, y, *kept = scan_forward(rot, zs, first, first_at, step, *params)
        squares = squares + rolled(swap(squares))
        q = lax.rsqrt(squares / inner_total + epsilon)
        q_col = q.reshape(2 * half, 1)
        branch = None
        if l < layers - 1:
            out_sent = (dot_nt(ghat[half:], w_out) * q_col[half:]).astype(bf16)
            ghat, out_sent = lax.optimization_barrier((ghat, out_sent))
            out_own = dot_nt(ghat[:half], w_out) * q_col[:half]
            out_own, out_got = lax.optimization_barrier((out_own, swap(out_sent)))
            branch = out_own + out_got.astype(f32)
        saved.append((hidden, scale, rows, zs, first, first_at, step, sig, params, ghat, y, kept, q, q_col, branch))
        if branch is not None:
            hidden = hidden + branch

    flow = cotangent
    summed = []
    large, early, late = [None] * layers, [None] * layers, [None] * layers
    for l in reversed(range(layers)):
        w_out = weights[l][-1]
        (
            hidden_in, scale, rows, zs, first, first_at, step, sig, params, ghat, y, kept, q, q_col,
            branch,
        ) = saved[l]
        flow_low = flow.astype(bf16)
        if l < layers - 1:
            part = jnp.sum(flow_low.astype(f32) * branch, axis=1).reshape(blocks // 2, 1, CHUNK)
            dots = jnp.concatenate([part, swap(part)], axis=0)
            go_got = swap(flow_low)
            go_got, last_sent, last_own = lax.optimization_barrier((go_got, last_sent, last_own))
            go = jnp.concatenate([flow_low, go_got], axis=0)
            qc = q * q * dots / inner_total
            last_got = swap(last_sent)
        else:
            go = jnp.concatenate([flow_low, swap(flow_low)], axis=0)
        go_scaled = (go.astype(f32) * q_col).astype(bf16)
        if l == 0:
            g_out = dot_tn(go_scaled, ghat).astype(bf16)
            go, g_out = lax.optimization_barrier((go, g_out))
            g_out = scatter_start(g_out)
            d_yn = dot_nn(go, w_out)
            z_sig = jax.nn.sigmoid(zs)
            d_gated = d_yn * params[-1] * q_col - y * (zs * z_sig) * qc.reshape(2 * half, 1)
            dz = (d_gated * y * (z_sig * (1.0 + zs * (1.0 - z_sig)))).astype(bf16)
            dz, g_out = lax.optimization_barrier((dz, g_out))
            g_z = dot_tn(rows, dz).astype(bf16)
            dz, g_z = lax.optimization_barrier((dz, g_z))
            g_z = scatter_start(g_z)
            d_part = dot_nt(dz[half:], weights[0][0])
            d_yn, g_out, g_z, d_part = lax.optimization_barrier((d_yn, g_out, g_z, d_part))
            g_pair = scatter_middle(g_out, g_z)
        else:
            d_yn = dot_nn(go, w_out)
            part = jnp.sum(d_yn * ghat.astype(f32), axis=1).reshape(blocks, 1, CHUNK)
            qc = q * q * q * (part + rolled(swap(part))) / inner_total
            g_out = dot_tn(go_scaled, ghat).astype(bf16)
            d_yn, g_out = lax.optimization_barrier((d_yn, g_out))
            g_out = scatter_plain(g_out)
        d_proj, gx, gs, gh = scan_backward(
            rot, l > 0, zs, first, first_at, step, sig, y, *kept, d_yn, q, qc, *params
        )
        if l == 0:
            d_proj = after(d_proj, last_got)
            g_first = after(dot_tn(rows, d_proj).astype(bf16), *summed)
            d_proj, g_first = lax.optimization_barrier((d_proj, g_first))
            g_pair = scatter_added(*g_pair, g_first)
            g_first = scatter_start(g_first)
            d_proj = after(d_proj, g_pair, g_first)
            d_sent = (dot_nt(d_proj[half:], weights[0][1]) + d_part).astype(bf16)
            d_proj, dz, d_sent = lax.optimization_barrier((d_proj, dz, d_sent))
            d_own = dot_nt(d_proj[:half], weights[0][1]) + dot_nt(dz[:half], weights[0][0])
        else:
            d_sent = dot_nt(d_proj[half:], weights[l][0]).astype(bf16)
            g_all = dot_tn(rows, after(d_proj, d_sent)).astype(bf16)
            d_proj, g_all = lax.optimization_barrier((d_proj, g_all))
            d_own = dot_nt(d_proj[:half], weights[l][0])
            ghat = after(ghat, g_all)
            last_sent = (dot_nt(ghat[half:], w_out) * q_col[half:]).astype(bf16)
            last_own = dot_nt(ghat[:half], w_out) * q_col[:half]
        d_got = swap(d_sent)
        if l == 0:
            g_pair = scatter_end(g_pair)
            g_first = scatter_added(*scatter_middle(g_first))
            d_got = after(d_got, g_first, g_pair)
            settled = g_first
            g_first, g_pair = scatter_end(g_first).astype(f32), after(g_pair, d_got).astype(f32)
            g_out, g_z = g_pair[:, :inner], g_pair[:, inner:]
        else:
            d_got, g_all = lax.optimization_barrier((d_got, g_all))
            g_all = after(g_all, g_out)
            g_out = g_out.astype(f32)
        d_own, d_got = lax.optimization_barrier((d_own, d_got))
        d_normed = d_own + d_got.astype(f32)
        weighted = d_normed * input_gain[l]
        g_gain = jnp.sum(d_normed * hidden_in * scale, axis=0).reshape(-1, LANES)
        inner_dot = jnp.sum(weighted * hidden_in, axis=1, keepdims=True)
        flow_next = flow + scale * weighted - hidden_in * (scale * scale * scale * inner_dot / width)
        flow = flow_next
        if l > 0:
            g_all = scatter_plain(after(g_all, flow))
            summed.append(g_all)
            g_all = g_all.astype(f32)
            g_z, g_first = g_all[:, :inner], g_all[:, inner:]
        g_bc = g_first[:, inner : inner + 2 * LANES]

        large[l] = (
            g_z, g_first[:, :inner], g_bc,
            g_first[:, inner + 2 * LANES : inner + 2 * LANES + heads], g_out.T,
        )
        early[l] = (gs[:5].reshape(-1, LANES), gx[:7].reshape(-1, LANES), gh[:2])
        late[l] = g_gain

    g_bc = jnp.stack([part[2] for part in large])
    bc_got = swap(lax.dynamic_slice_in_dim(g_bc, (1 - mine) * bc_rows, bc_rows, 1))
    g_bc = lax.dynamic_slice_in_dim(g_bc, mine * bc_rows, bc_rows, 1) + bc_got
    hidden = hidden + (last_own + after(last_got, settled).astype(f32))
    shared = jnp.concatenate([e[0] for e in early] + late, axis=0)
    shared = shared + swap(shared)
    small = butterfly(jnp.concatenate([shared] + [part for e in early for part in e[1:]], axis=0))
    at = 0

    def take(*shape):
        nonlocal at
        size = 1
        for s in shape:
            size *= s
        at += size // LANES
        return small[at - size // LANES : at].reshape(shape)

    r_state = jnp.stack([take(5, 2 * LANES) for _ in range(layers)])
    r_gain = jnp.stack([take(width) for _ in range(layers)])
    r_inner, r_head = zip(*[(take(7, inner), take(2, LANES)) for _ in range(layers)])
    r_inner, r_head = jnp.stack(r_inner), jnp.stack(r_head)[:, :, :heads]
    g_z, g_x, _, g_dt, g_out = (jnp.stack(parts) for parts in zip(*large))
    return (
        hidden, flow, r_gain, g_z, g_x, g_bc, g_dt,
        r_inner[:, :4], r_inner[:, 4], r_state[:, :4], r_state[:, 4],
        r_head[:, 0], r_head[:, 1],
        jnp.sum(r_inner[:, 5].reshape(layers, heads, HEADDIM), axis=2), r_inner[:, 6], g_out,
    )


def solution(mesh):
    row = P(("dp", "tensor"), None)
    rest = (
        P(), P(None, "dp", "tensor"), P(None, "dp", "tensor"), P(None, ("dp", "tensor"), None),
        P(None, "dp", "tensor"), P(None, None, "tensor"), P(None, "tensor"), P(), P(),
        P(None, "tensor"), P(None, "tensor"), P(None, "tensor"), P(None, "tensor"),
        P(None, "tensor", "dp"),
    )
    specs = (row, row, *rest)
    return jax.shard_map(local, mesh=mesh, in_specs=specs, out_specs=specs, check_vma=False)
```

```python
import functools

import jax
import jax.numpy as jnp
from jax import lax
from jax.experimental import pallas as pl
from jax.experimental.pallas import tpu as pltpu
from jax.sharding import PartitionSpec as P

HEADDIM = 64
CHUNK = 128
LANES = 128
WIDE = 256
epsilon = 1e-05
f32 = jnp.float32
bf16 = jnp.bfloat16


def dot_nn(left, right):
    return lax.dot_general(left, right, (((1,), (0,)), ((), ())), preferred_element_type=f32)


def dot_nt(left, right):
    return lax.dot_general(left, right, (((1,), (1,)), ((), ())), preferred_element_type=f32)


def dot_tn(left, right):
    return lax.dot_general(left, right, (((0,), (0,)), ((), ())), preferred_element_type=f32)


def conv_rows(ext, kernel, offset, length):
    total = offset + kernel[0:1] * ext[5 : 5 + length]
    for tap in range(1, 4):
        total = total + kernel[tap : tap + 1] * ext[5 + tap : 5 + tap + length]
    return total


def row_col(size):
    return (
        lax.broadcasted_iota(jnp.int32, (size, size), 0),
        lax.broadcasted_iota(jnp.int32, (size, size), 1),
    )


def decays(dt_ref, rate_ref, lower):
    step = dt_ref[...]
    lower = lower.astype(bf16)
    cum = dot_nn(jnp.concatenate([lower] * 3, axis=1), three_parts(step * rate_ref[...]))
    last = cum[CHUNK - 1 : CHUNK]
    return step, cum, cum.T, last, jnp.exp(cum), jnp.exp(last - cum)


def two_parts(values, axis):
    high = values.astype(bf16)
    return jnp.concatenate([high, (values - high.astype(f32)).astype(bf16)], axis=axis)


def three_parts(values):
    high = values.astype(bf16)
    rest = values - high.astype(f32)
    middle = rest.astype(bf16)
    return jnp.concatenate([high, middle, (rest - middle.astype(f32)).astype(bf16)], axis=0)


def heads_of(channels, axis):
    shape = (channels, LANES) if axis == 0 else (LANES, channels)
    at = lax.broadcasted_iota(jnp.int32, shape, axis)
    head = lax.broadcasted_iota(jnp.int32, shape, 1 - axis)
    return jnp.where((at >= head * HEADDIM) & (at < (head + 1) * HEADDIM), 1.0, 0.0).astype(bf16)


def block_diagonal(values, low_half):
    zero = jnp.zeros_like(values)
    return jnp.concatenate(
        [jnp.where(low_half, values, zero), jnp.where(low_half, zero, values)], axis=0
    )


def forward_kernel(
    rot_ref, xr_ref, bcr_ref, dt_ref, zr_ref,
    cw_ref, cb_ref, sw_ref, sb_ref, rate_ref, skip_ref, gain_ref,
    ghat_ref, ssq_ref, y_ref, s_ref, pre_ref, bc_pre_ref,
    state, x_halo, bc_halo, widen, wide,
):
    @pl.when(pl.program_id(0) == 0)
    def _():
        widen[...] = jnp.concatenate([heads_of(xr_ref.shape[1], 1)] * 2, axis=0)
        state[...] = jnp.zeros_like(state)
        x_halo[...] = jnp.zeros_like(x_halo)
        bc_halo[...] = jnp.zeros_like(bc_halo)

    rows, cols = row_col(CHUNK)
    causal = rows >= cols
    low_half = cols < HEADDIM
    step, cum, cum_t, last, grow, tail = decays(dt_ref, rate_ref, jnp.where(causal, 1.0, 0.0))
    wide[...] = dot_nn(two_parts(jnp.concatenate([step, grow, tail], axis=0), 1), widen[...])
    last_grow = jnp.exp(last)
    bc_ext = jnp.concatenate([bc_halo[...], bcr_ref[...]], axis=0)
    bc_halo[...] = bcr_ref[CHUNK - 8 :]
    bc_pre = conv_rows(bc_ext, sw_ref[...], sb_ref[...], CHUNK)
    bc_pre_ref[...] = bc_pre
    bc = (bc_pre * jax.nn.sigmoid(bc_pre)).astype(bf16)
    b_low, c_low = bc[:, :LANES], bc[:, LANES:]
    b_turned = b_low.astype(f32).T.astype(bf16)
    mix = jnp.where(causal, dot_nt(c_low, b_low), 0.0)
    squares = jnp.zeros((CHUNK, LANES), f32)

    def spread(cols_of, quad):
        low = low_half[: cols_of.shape[0]]
        return jnp.concatenate(
            [
                jnp.where(low, cols_of[:, h : h + 1], cols_of[:, h + 1 : h + 2])
                for h in (4 * quad, 4 * quad + 2)
            ],
            axis=1,
        )

    for quad in range(xr_ref.shape[1] // WIDE):
        at = slice(quad * WIDE, (quad + 1) * WIDE)
        xr = xr_ref[:, at]
        behind = x_halo[:, at]
        x_halo[:, at] = xr[CHUNK - 8 :]
        strips = []
        for strip in range(0, CHUNK, 8):
            here = xr[strip : strip + 8]
            both = jnp.concatenate([behind, here], axis=0)
            total = cb_ref[:, at] + cw_ref[3:4, at] * here
            for tap in range(3):
                total = total + cw_ref[tap : tap + 1, at] * both[5 + tap : 13 + tap]
            strips.append(total)
            behind = here
        pre = jnp.concatenate(strips, axis=0)
        pre_ref[:, at] = pre
        x = (pre * jax.nn.sigmoid(pre)).astype(bf16).astype(f32)
        x_stepped = x * wide[:CHUNK, at]
        x_step = x_stepped.astype(bf16)
        s_in = state[:, at]
        s_low = s_in.astype(bf16)
        s_ref[0, :, at] = s_low
        parts = []
        for pair in range(2):
            mixed = []
            for h in range(4 * quad + 2 * pair, 4 * quad + 2 * pair + 2):
                decay = jnp.exp(jnp.minimum(cum[:, h : h + 1] - cum_t[h : h + 1, :], 0.0))
                mixed.append((mix * decay).astype(bf16))
            right = block_diagonal(x_step[:, pair * LANES : (pair + 1) * LANES], low_half)
            parts.append(dot_nn(jnp.concatenate(mixed, axis=1), right))
        across = dot_nn(c_low, s_low) * wide[CHUNK : 2 * CHUNK, at]
        y = jnp.concatenate(parts, axis=1) + across + skip_ref[:, at] * x
        y_ref[:, at] = y
        z = zr_ref[:, at]
        gated = y * (z * jax.nn.sigmoid(z))
        squared = gated * gated
        squares = squares + (squared[:, :LANES] + squared[:, LANES:])
        ghat_ref[:, at] = (gated * gain_ref[:, at]).astype(bf16)
        fresh = dot_nn(b_turned, (x_stepped * wide[2 * CHUNK :, at]).astype(bf16))
        state[:, at] = s_in * spread(last_grow, quad) + fresh
    ssq_ref[0] = jnp.sum(squares.T, axis=0, keepdims=True)


def backward_kernel(
    gate_at, x_at, rot_ref, xr_ref, pre_ref, bcr_ref, bc_pre_ref, dt_ref, sig_ref, zr_ref, y_ref, s_ref, dyn_ref, q_ref, qc_ref,
    cw_ref, sw_ref, rate_ref, skip_ref, gain_ref,
    dp_ref, gx_ref, gs_ref, gh_ref,
    dstate, x_halo, bc_halo, narrow, products, crossings, gx_parts, gs_parts, gh_parts,
):
    inner = xr_ref.shape[1]
    first = pl.program_id(0) == pl.num_programs(0) - 1

    @pl.when(pl.program_id(0) == 0)
    def _():
        dstate[...] = jnp.zeros_like(dstate)
        x_halo[...] = jnp.zeros_like(x_halo)
        bc_halo[...] = jnp.zeros_like(bc_halo)
        narrow[...] = heads_of(inner, 0)
        gx_parts[...] = jnp.zeros_like(gx_parts)
        gs_parts[...] = jnp.zeros_like(gs_parts)
        gh_parts[...] = jnp.zeros_like(gh_parts)

    rows, cols = row_col(CHUNK)
    upper = cols >= rows
    low_half = cols < HEADDIM
    step, cum, cum_t, last, grow, tail = decays(dt_ref, rate_ref, jnp.where(rows >= cols, 1.0, 0.0))
    last_grow = jnp.exp(last)
    bcr = bcr_ref[...]
    bc_pre = bc_pre_ref[...]
    bc_sig = jax.nn.sigmoid(bc_pre)
    bc = (bc_pre * bc_sig).astype(bf16)
    b_low, c_low = bc[:, :LANES], bc[:, LANES:]
    c_turned = c_low.astype(f32).T.astype(bf16)
    mix = jnp.where(upper, dot_nt(b_low, c_low), 0.0)
    q = jnp.broadcast_to(q_ref[0], (WIDE, CHUNK)).T
    qc = jnp.broadcast_to(qc_ref[0], (WIDE, CHUNK)).T

    def spread(cols_of, quad):
        low = low_half[: cols_of.shape[0]]
        return jnp.concatenate(
            [
                jnp.where(low, cols_of[:, h : h + 1], cols_of[:, h + 1 : h + 2])
                for h in (4 * quad, 4 * quad + 2)
            ],
            axis=1,
        )

    def add_to(parts, index, at, values):
        parts[8 * index : 8 * index + 8, at] += jnp.sum(
            values.reshape(CHUNK // 8, 8, values.shape[1]), axis=0
        )

    d_mix = jnp.zeros((CHUNK, CHUNK), f32)
    d_b = jnp.zeros((CHUNK, LANES), f32)
    d_c = jnp.zeros((CHUNK, LANES), f32)
    for quad in range(inner // WIDE):
        at = slice(quad * WIDE, (quad + 1) * WIDE)
        xr = xr_ref[:, at]
        pre = pre_ref[:, at]
        sig = jax.nn.sigmoid(pre)
        x_low = (pre * sig).astype(bf16)
        x = x_low.astype(f32)
        step_wide = spread(step, quad)
        x_stepped = x * step_wide
        x_step = x_stepped.astype(bf16)
        z = zr_ref[:, at]
        z_sig = jax.nn.sigmoid(z)
        z_act = z * z_sig
        y = y_ref[:, at]
        gated = y * z_act
        dyn = dyn_ref[:, at]
        add_to(gx_parts, 6, at, dyn * gated * q)
        d_gated = dyn * (gain_ref[:, at] * q) - gated * qc
        if gate_at is not None:
            dp_ref[:, at] = (d_gated * y * (z_sig * (1.0 + z * (1.0 - z_sig)))).astype(bf16)
        dy = d_gated * z_act
        dy_low = dy.astype(bf16)
        dy_wide = dy_low.astype(f32)
        add_to(gx_parts, 5, at, dy * x)
        ds = dstate[:, at]
        ds_low = ds.astype(bf16)
        parts = []
        for pair in range(2):
            half = slice(pair * LANES, (pair + 1) * LANES)
            own = [
                jnp.exp(jnp.minimum(cum_t[h : h + 1, :] - cum[:, h : h + 1], 0.0))
                for h in range(4 * quad + 2 * pair, 4 * quad + 2 * pair + 2)
            ]
            right = block_diagonal(dy_low[:, half], low_half)
            mixed = jnp.concatenate([(mix * decay).astype(bf16) for decay in own], axis=1)
            parts.append(dot_nn(mixed, right))
            d_mixed = dot_nt(x_step[:, half], right)
            d_mix = d_mix + d_mixed[:, :CHUNK] * own[0] + d_mixed[:, CHUNK:] * own[1]
        within = jnp.concatenate(parts, axis=1)
        tail_wide = spread(tail, quad)
        beyond = dot_nn(b_low, ds_low) * tail_wide
        skip = skip_ref[:, at]
        dx = step_wide * (within + beyond) + skip * dy
        moved = dy_wide * (y - skip * x) - x_step.astype(f32) * within
        products[: 2 * CHUNK, at] = two_parts(moved, 0)
        products[2 * CHUNK : 3 * CHUNK, at] = (x * within).astype(bf16)
        products[3 * CHUNK :, at] = (x * beyond).astype(bf16)
        s_low = s_ref[0, :, at]
        crossings[:, at] = jnp.sum(
            (ds * s_low.astype(f32)).reshape(CHUNK // 8, 8, WIDE), axis=0
        )
        dy_grow = (dy_wide * spread(grow, quad)).astype(bf16)
        d_c = d_c + dot_nt(dy_grow, s_low)
        d_b = d_b + dot_nt((x_stepped * tail_wide).astype(bf16), ds_low)
        dstate[:, at] = ds * spread(last_grow, quad) + dot_nn(c_turned, dy_grow)
        d_pre = dx * (sig * (1.0 + pre * (1.0 - sig)))
        d_ext = jnp.concatenate([d_pre, x_halo[:, at]], axis=0)
        x_halo[:, at] = d_pre[:8]
        d_raw = cw_ref[3:4, at] * d_pre
        for tap in range(3):
            moved = d_ext[3 - tap : 3 - tap + CHUNK]
            d_raw = d_raw + cw_ref[tap : tap + 1, at] * moved
            add_to(gx_parts, tap, at, moved * xr)
        add_to(gx_parts, 3, at, d_pre * xr)
        add_to(gx_parts, 4, at, d_pre)
        dp_ref[:, x_at + at.start : x_at + at.stop] = d_raw.astype(bf16)
    d_mix = jnp.where(upper, d_mix, 0.0)
    d_b = d_b + dot_nn(d_mix.astype(bf16), c_low)
    d_c = d_c + dot_nn(d_mix.T.astype(bf16), b_low)
    d_bc = jnp.concatenate([d_b, d_c], axis=1)
    d_pre = d_bc * (bc_sig * (1.0 + bc_pre * (1.0 - bc_sig)))
    d_ext = jnp.concatenate([d_pre, bc_halo[...]], axis=0)
    bc_halo[...] = d_pre[:8]
    d_raw = sw_ref[3:4] * d_pre
    whole = slice(None)
    for tap in range(3):
        moved = d_ext[3 - tap : 3 - tap + CHUNK]
        d_raw = d_raw + sw_ref[tap : tap + 1] * moved
        add_to(gs_parts, tap, whole, moved * bcr)
    add_to(gs_parts, 3, whole, d_pre * bcr)
    add_to(gs_parts, 4, whole, d_pre)
    dp_ref[:, x_at + inner : x_at + inner + 2 * LANES] = d_raw.astype(bf16)
    sums = dot_nn(products[...], narrow[...])
    d_cum = sums[:CHUNK] + sums[CHUNK : 2 * CHUNK]
    d_beyond = sums[3 * CHUNK :]
    through = jnp.sum(dot_nn(two_parts(crossings[...], 0), narrow[...]), axis=0, keepdims=True)
    later = jnp.where(upper, 1.0, 0.0).astype(bf16)
    d_log = through * last_grow + dot_nn(
        jnp.concatenate([later] * 3 + [1 - later] * 3, axis=1),
        jnp.concatenate([three_parts(d_cum), three_parts(step * d_beyond)], axis=0),
    )
    rate = rate_ref[...]
    d_raw_step = (d_log * rate + sums[2 * CHUNK : 3 * CHUNK] + d_beyond) * sig_ref[...]
    add_to(gh_parts, 0, whole, d_raw_step)
    add_to(gh_parts, 1, whole, d_log * step * rate)
    dp_ref[:, x_at + inner + 2 * LANES :] = d_raw_step.astype(bf16)

    @pl.when(first)
    def _():
        for parts, ref in ((gx_parts, gx_ref), (gs_parts, gs_ref), (gh_parts, gh_ref)):
            width = ref.shape[1]
            ref[...] = jnp.sum(parts[...].reshape(8, 8, width), axis=1)


def in_hbm(*arrays):
    return [pltpu.with_memory_space_constraint(array, pltpu.HBM) for array in arrays]


def whole_spec(array):
    return pl.BlockSpec(array.shape, lambda c, rot: (0,) * array.ndim)


def rows_kernel(rows_ref, weight_ref, *refs):
    refs[-1][...] = dot_nn(rows_ref[...], weight_ref[...])


def rows_product(rows, weight, tile, into=None):
    height, depth = rows.shape
    columns = weight.shape[1]
    place = 0 if into is None else 1
    specs = [
        pl.BlockSpec((height, depth), lambda j: (0, 0)),
        pl.BlockSpec((depth, tile), lambda j: (0, j)),
    ]
    rest = () if into is None else (into,)
    return pl.pallas_call(
        rows_kernel,
        grid=(columns // tile,),
        in_specs=specs + [pl.BlockSpec(memory_space=pl.ANY)] * len(rest),
        out_specs=pl.BlockSpec((height, tile), lambda j: (place, j)),
        out_shape=pltpu.HBM((2 * height, columns), f32),
        input_output_aliases={2: 0} if rest else {},
        compiler_params=pltpu.CompilerParams(
            dimension_semantics=("arbitrary",), vmem_limit_bytes=24 * 2**20
        ),
        cost_estimate=pl.CostEstimate(
            flops=2 * height * depth * columns,
            bytes_accessed=2 * depth * columns + 4 * height * columns,
            transcendentals=0,
        ),
        name="rows_product",
    )(rows, *in_hbm(weight), *rest)


def scan_forward(rot, zs, first, first_at, step, conv, conv_bias, conv_s, conv_s_bias, rate, skip, gain):
    length, inner = zs.shape[0], gain.shape[1]
    blocks = length // CHUNK

    def place(width, column=0):
        return pl.BlockSpec((CHUNK, width), lambda c, rot: ((c + rot[0]) % blocks, column))

    params = (conv, conv_bias, conv_s, conv_s_bias, rate, skip, gain)
    return pl.pallas_call(
        forward_kernel,
        grid_spec=pltpu.PrefetchScalarGridSpec(
            num_scalar_prefetch=1,
            grid=(blocks,),
            in_specs=[
                place(inner, first_at // inner), place(2 * LANES, (first_at + inner) // (2 * LANES)), place(LANES), place(inner),
                *map(whole_spec, params),
            ],
            out_specs=[
                place(inner),
                pl.BlockSpec((1, 1, CHUNK), lambda c, rot: ((c + rot[0]) % blocks, 0, 0)),
                place(inner),
                pl.BlockSpec((1, LANES, inner), lambda c, rot: (c, 0, 0)),
                place(inner), place(2 * LANES),
            ],
            scratch_shapes=[
                pltpu.VMEM((LANES, inner), f32),
                pltpu.VMEM((8, inner), f32),
                pltpu.VMEM((8, 2 * LANES), f32),
                pltpu.VMEM((2 * LANES, inner), bf16),
                pltpu.VMEM((3 * CHUNK, inner), f32),
            ],
        ),
        out_shape=[
            pltpu.HBM((length, inner), bf16),
            jax.ShapeDtypeStruct((blocks, 1, CHUNK), f32),
            pltpu.HBM((length, inner), f32),
            pltpu.HBM((blocks, LANES, inner), bf16),
            pltpu.HBM((length, inner), f32),
            pltpu.HBM((length, 2 * LANES), f32),
        ],
        compiler_params=pltpu.CompilerParams(
            dimension_semantics=("arbitrary",), vmem_limit_bytes=20 * 2**20
        ),
        cost_estimate=pl.CostEstimate(
            flops=int(25e9), bytes_accessed=25 * 2**20, transcendentals=0
        ),
        name="scan_forward",
    )(rot, *in_hbm(first, first), step, *in_hbm(zs), *params)


def scan_backward(
    rot, with_gate, zs, first, first_at, step, sig, y, states, pre, bc_pre, d_yn, q, qc,
    conv, conv_bias, conv_s, conv_s_bias, rate, skip, gain,
):
    length, inner = zs.shape[0], gain.shape[1]
    blocks = length // CHUNK

    def place(width, column=0):
        return pl.BlockSpec(
            (CHUNK, width), lambda c, rot: ((blocks - 1 - c + rot[0]) % blocks, column)
        )

    def fixed(height, width):
        return pl.BlockSpec((height, width), lambda c, rot: (0, 0))

    line = pl.BlockSpec(
        (1, 1, CHUNK), lambda c, rot: ((blocks - 1 - c + rot[0]) % blocks, 0, 0)
    )
    params = (conv, conv_s, rate, skip, gain)
    x_at, bc_at = first_at // inner, (first_at + inner) // (2 * LANES)
    out_width = (2 if with_gate else 1) * inner + 3 * LANES
    kernel = functools.partial(
        backward_kernel, 0 if with_gate else None, inner if with_gate else 0
    )
    return pl.pallas_call(
        kernel,
        grid_spec=pltpu.PrefetchScalarGridSpec(
            num_scalar_prefetch=1,
            grid=(blocks,),
            in_specs=[
                place(inner, x_at), place(inner), place(2 * LANES, bc_at), place(2 * LANES),
                place(LANES), place(LANES), place(inner), place(inner),
                pl.BlockSpec((1, LANES, inner), lambda c, rot: (blocks - 1 - c, 0, 0)),
                place(inner), line, line,
                *map(whole_spec, params),
            ],
            out_specs=[
                place(out_width),
                fixed(8, inner), fixed(8, 2 * LANES), fixed(8, LANES),
            ],
            scratch_shapes=[
                pltpu.VMEM((LANES, inner), f32),
                pltpu.VMEM((8, inner), f32),
                pltpu.VMEM((8, 2 * LANES), f32),
                pltpu.VMEM((inner, LANES), bf16),
                pltpu.VMEM((4 * CHUNK, inner), bf16),
                pltpu.VMEM((8, inner), f32),
                pltpu.VMEM((64, inner), f32),
                pltpu.VMEM((64, 2 * LANES), f32),
                pltpu.VMEM((64, LANES), f32),
            ],
        ),
        out_shape=[
            pltpu.HBM((length, out_width), bf16),
            jax.ShapeDtypeStruct((8, inner), f32),
            jax.ShapeDtypeStruct((8, 2 * LANES), f32),
            jax.ShapeDtypeStruct((8, LANES), f32),
        ],
        compiler_params=pltpu.CompilerParams(
            dimension_semantics=("arbitrary",), vmem_limit_bytes=28 * 2**20
        ),
        cost_estimate=pl.CostEstimate(
            flops=int(10e9), bytes_accessed=40 * 2**20, transcendentals=0
        ),
        name="scan_backward",
    )(rot, *in_hbm(first, pre, first, bc_pre), step, sig, *in_hbm(zs, y, states, d_yn), q, qc, *params)


TENSOR_SWAP = [(0, 1), (1, 0)]


def swap(values):
    return lax.ppermute(values, "tensor", TENSOR_SWAP)


def butterfly(values):
    size = lax.axis_size("dp")
    step = 1
    while step < size:
        values = values + lax.ppermute(values, "dp", [(i, i ^ step) for i in range(size)])
        step *= 2
    return values


LINE, SIDE, CORE = 4, 2, 2
PLACES = [(z, x, c) for z in range(LINE) for x in range(SIDE) for c in range(CORE)]


def index_of(z, x, c):
    return (z * SIDE + x) * CORE + c


def along_line(step, lowest, highest_place):
    return [
        (index_of(z, x, c), index_of(z + step, x, c))
        for z, x, c in PLACES
        if lowest <= z <= highest_place
    ]


OTHER_SIDE = [(index_of(z, x, c), index_of(z, 1 - x, c)) for z, x, c in PLACES]
OTHER_CORE = [(index_of(z, x, c), index_of(z, x, 1 - c)) for z, x, c in PLACES]
LINES = [[index_of(z, x, c) for z in range(LINE)] for x in range(SIDE) for c in range(CORE)]


def place_of():
    at = lax.axis_index("dp")
    return at // (SIDE * CORE), (at // CORE) % SIDE, at % CORE


def paired(own, other, mine, axis):
    return jnp.where(
        mine == 0, jnp.stack([own, other], axis=axis), jnp.stack([other, own], axis=axis)
    )


def gather_start(shard):
    if lax.axis_size("dp") != LINE * SIDE * CORE:
        return (lax.all_gather(shard, "dp", axis=0, tiled=True),)
    z = place_of()[0]
    rows, columns = shard.shape
    right, left = [shard], [shard]
    for step in range(1, LINE):
        right.append(lax.ppermute(right[-1], "dp", along_line(1, step - 1, LINE - 2)))
        left.append(lax.ppermute(left[-1], "dp", along_line(-1, 1, LINE - step)))
    line = jnp.concatenate(right[:0:-1] + left, axis=0)
    line = lax.dynamic_slice_in_dim(line, (LINE - 1 - z) * rows, LINE * rows, 0)
    line = line.reshape(LINE, rows, columns)
    return line, lax.ppermute(line, "dp", OTHER_SIDE)


def gather_end(lines):
    if lax.axis_size("dp") != LINE * SIDE * CORE:
        return lines[0]
    _, x, c = place_of()
    pair = paired(*lines, x, 1)
    full = paired(pair, lax.ppermute(pair, "dp", OTHER_CORE), c, 2)
    return full.reshape(-1, full.shape[-1])


def part_of(blocks, at, axis):
    return lax.dynamic_index_in_dim(blocks, at, axis, keepdims=False)


def added(kept, got):
    return (kept.astype(f32) + got.astype(f32)).astype(bf16)


def scatter_start(values):
    if lax.axis_size("dp") != LINE * SIDE * CORE:
        return values
    c = place_of()[2]
    blocks = values.reshape(LINE, SIDE, CORE, -1, values.shape[1])
    got = lax.ppermute(part_of(blocks, 1 - c, 2), "dp", OTHER_CORE)
    return added(part_of(blocks, c, 2), got)


def scatter_middle(*blocks):
    if lax.axis_size("dp") != LINE * SIDE * CORE:
        return jnp.concatenate(blocks, axis=1), None
    x = place_of()[1]
    sent = jnp.concatenate([part_of(b, 1 - x, 1) for b in blocks], axis=-1)
    kept = jnp.concatenate([part_of(b, x, 1) for b in blocks], axis=-1)
    return kept, lax.ppermute(sent, "dp", OTHER_SIDE)


def scatter_added(kept, got, *earlier):
    return kept if got is None else added(kept, after(got, *earlier))


def scatter_end(blocks):
    if lax.axis_size("dp") != LINE * SIDE * CORE:
        return scatter_plain(blocks)
    return lax.psum_scatter(
        blocks.reshape(-1, blocks.shape[-1]), "dp", scatter_dimension=0, tiled=True,
        axis_index_groups=LINES,
    )


def after(values, *earlier):
    return lax.optimization_barrier((values, *earlier))[0]


def gather_plain(shard):
    return lax.all_gather(shard, "dp", axis=0, tiled=True)


def scatter_plain(values):
    return lax.psum_scatter(values, "dp", scatter_dimension=0, tiled=True)


def rolled(values):
    half = values.shape[0] // 2
    return jnp.concatenate([values[half:], values[:half]], axis=0)


def pad_lanes(values):
    return jnp.pad(values, ((0, 0), (0, LANES - values.shape[1])))


def local(
    residual_in, cotangent, input_gain, z_weight, x_weight, bc_weight, dt_weight,
    conv_inner, conv_inner_bias, conv_state, conv_state_bias, dt_bias, decay_log,
    skip_gain, gated_gain, out_weight,
):
    layers = input_gain.shape[0]
    half, width = residual_in.shape
    inner = gated_gain.shape[1]
    heads = dt_bias.shape[1]
    inner_total = inner * lax.axis_size("tensor")
    blocks = 2 * half // CHUNK
    bc_rows = bc_weight.shape[1]
    mine = lax.axis_index("tensor")
    rot = (mine * (blocks // 2)).astype(jnp.int32).reshape(1)

    bc_other = swap(bc_weight)
    bc_pair = jnp.where(
        mine == 0,
        jnp.concatenate([bc_weight, bc_other], axis=1),
        jnp.concatenate([bc_other, bc_weight], axis=1),
    )

    def first_shard(l):
        return jnp.concatenate([x_weight[l], bc_pair[l], pad_lanes(dt_weight[l])], axis=1)

    def project(rows, l):
        if l == 0:
            lines, w_first, w_out = weights[0]
            rows = jnp.concatenate(rows, axis=0)
            first = dot_nn(rows, w_first)
            w_z = gather_end((*lines[:-1], after(lines[-1], first)))
            weights[0] = (w_z, w_first, w_out)
            return dot_nn(rows, w_z), first, 0
        both = rows_product(rows[0], weights[l][0], 9 * LANES)
        both = rows_product(rows[1], weights[l][0], 9 * LANES, both)
        return both, both, inner

    weights = [(gather_start(z_weight[0]), gather_plain(first_shard(0)), gather_plain(out_weight[0].T))]
    for l in range(1, layers):
        both = jnp.concatenate([z_weight[l], first_shard(l)], axis=1)
        weights.append((gather_plain(both), gather_plain(out_weight[l].T)))

    def params_of(l):
        rate = pad_lanes(-jnp.exp(decay_log[l])[None])
        return (
            conv_inner[l], conv_inner_bias[l][None], conv_state[l], conv_state_bias[l][None],
            rate, jnp.repeat(skip_gain[l], HEADDIM)[None], gated_gain[l][None],
        )

    saved = []
    hidden = residual_in
    for l in range(layers):
        w_out = weights[l][-1]
        scale = lax.rsqrt(jnp.mean(hidden * hidden, axis=1, keepdims=True) + epsilon)
        normed = (hidden * scale * input_gain[l]).astype(bf16)
        halves = (normed, swap(normed))
        zs, first, first_at = project(halves, l)
        rows = jnp.concatenate(halves, axis=0)
        raw_step = first[:, first_at + inner + 2 * LANES :] + pad_lanes(dt_bias[l][None])
        step = jax.nn.softplus(raw_step)
        sig = jax.nn.sigmoid(raw_step)
        params = params_of(l)
        ghat, squares, y, *kept = scan_forward(rot, zs, first, first_at, step, *params)
        squares = squares + rolled(swap(squares))
        q = lax.rsqrt(squares / inner_total + epsilon)
        q_col = q.reshape(2 * half, 1)
        branch = None
        if l < layers - 1:
            out_sent = (dot_nt(ghat[half:], w_out) * q_col[half:]).astype(bf16)
            ghat, out_sent = lax.optimization_barrier((ghat, out_sent))
            out_own = dot_nt(ghat[:half], w_out) * q_col[:half]
            out_own, out_got = lax.optimization_barrier((out_own, swap(out_sent)))
            branch = out_own + out_got.astype(f32)
        saved.append((hidden, scale, rows, zs, first, first_at, step, sig, params, ghat, y, kept, q, q_col, branch))
        if branch is not None:
            hidden = hidden + branch

    flow = cotangent
    summed = []
    large, early, late = [None] * layers, [None] * layers, [None] * layers
    for l in reversed(range(layers)):
        w_out = weights[l][-1]
        (
            hidden_in, scale, rows, zs, first, first_at, step, sig, params, ghat, y, kept, q, q_col,
            branch,
        ) = saved[l]
        flow_low = flow.astype(bf16)
        if l < layers - 1:
            part = jnp.sum(flow_low.astype(f32) * branch, axis=1).reshape(blocks // 2, 1, CHUNK)
            dots = jnp.concatenate([part, swap(part)], axis=0)
            go_got = swap(flow_low)
            go_got, last_sent, last_own = lax.optimization_barrier((go_got, last_sent, last_own))
            go = jnp.concatenate([flow_low, go_got], axis=0)
            qc = q * q * dots / inner_total
            last_got = swap(last_sent)
        else:
            go = jnp.concatenate([flow_low, swap(flow_low)], axis=0)
        go_scaled = (go.astype(f32) * q_col).astype(bf16)
        if l == 0:
            g_out = dot_tn(go_scaled, ghat).astype(bf16)
            go, g_out = lax.optimization_barrier((go, g_out))
            g_out = scatter_start(g_out)
            d_yn = dot_nn(go, w_out)
            z_sig = jax.nn.sigmoid(zs)
            d_gated = d_yn * params[-1] * q_col - y * (zs * z_sig) * qc.reshape(2 * half, 1)
            dz = (d_gated * y * (z_sig * (1.0 + zs * (1.0 - z_sig)))).astype(bf16)
            dz, g_out = lax.optimization_barrier((dz, g_out))
            g_z = dot_tn(rows, dz).astype(bf16)
            dz, g_z = lax.optimization_barrier((dz, g_z))
            g_z = scatter_start(g_z)
            d_part = dot_nt(dz[half:], weights[0][0])
            d_yn, g_out, g_z, d_part = lax.optimization_barrier((d_yn, g_out, g_z, d_part))
            g_pair = scatter_middle(g_out, g_z)
        else:
            d_yn = dot_nn(go, w_out)
            part = jnp.sum(d_yn * ghat.astype(f32), axis=1).reshape(blocks, 1, CHUNK)
            qc = q * q * q * (part + rolled(swap(part))) / inner_total
            g_out = dot_tn(go_scaled, ghat).astype(bf16)
            d_yn, g_out = lax.optimization_barrier((d_yn, g_out))
            g_out = scatter_plain(g_out)
        d_proj, gx, gs, gh = scan_backward(
            rot, l > 0, zs, first, first_at, step, sig, y, *kept, d_yn, q, qc, *params
        )
        if l == 0:
            d_proj = after(d_proj, last_got)
            g_first = after(dot_tn(rows, d_proj).astype(bf16), *summed)
            d_proj, g_first = lax.optimization_barrier((d_proj, g_first))
            g_pair = scatter_added(*g_pair, g_first)
            g_first = scatter_start(g_first)
            d_proj = after(d_proj, g_pair, g_first)
            d_sent = (dot_nt(d_proj[half:], weights[0][1]) + d_part).astype(bf16)
            d_proj, dz, d_sent = lax.optimization_barrier((d_proj, dz, d_sent))
            d_own = dot_nt(d_proj[:half], weights[0][1]) + dot_nt(dz[:half], weights[0][0])
        else:
            d_sent = dot_nt(d_proj[half:], weights[l][0]).astype(bf16)
            g_all = dot_tn(rows, after(d_proj, d_sent)).astype(bf16)
            d_proj, g_all = lax.optimization_barrier((d_proj, g_all))
            d_own = dot_nt(d_proj[:half], weights[l][0])
            ghat = after(ghat, g_all)
            last_sent = (dot_nt(ghat[half:], w_out) * q_col[half:]).astype(bf16)
            last_own = dot_nt(ghat[:half], w_out) * q_col[:half]
        d_got = swap(d_sent)
        if l == 0:
            g_pair = scatter_end(g_pair)
            g_first = scatter_added(*scatter_middle(g_first))
            d_got = after(d_got, g_first, g_pair)
            settled = g_first
            g_first, g_pair = scatter_end(g_first).astype(f32), after(g_pair, d_got).astype(f32)
            g_out, g_z = g_pair[:, :inner], g_pair[:, inner:]
        else:
            d_got, g_all = lax.optimization_barrier((d_got, g_all))
            g_all = after(g_all, g_out)
            g_out = g_out.astype(f32)
        d_own, d_got = lax.optimization_barrier((d_own, d_got))
        d_normed = d_own + d_got.astype(f32)
        weighted = d_normed * input_gain[l]
        g_gain = jnp.sum(d_normed * hidden_in * scale, axis=0).reshape(-1, LANES)
        inner_dot = jnp.sum(weighted * hidden_in, axis=1, keepdims=True)
        flow_next = flow + scale * weighted - hidden_in * (scale * scale * scale * inner_dot / width)
        flow = flow_next
        if l > 0:
            g_all = scatter_plain(after(g_all, flow))
            summed.append(g_all)
            g_all = g_all.astype(f32)
            g_z, g_first = g_all[:, :inner], g_all[:, inner:]
        g_bc = g_first[:, inner : inner + 2 * LANES]

        large[l] = (
            g_z, g_first[:, :inner], g_bc,
            g_first[:, inner + 2 * LANES : inner + 2 * LANES + heads], g_out.T,
        )
        early[l] = (gs[:5].reshape(-1, LANES), gx[:7].reshape(-1, LANES), gh[:2])
        late[l] = g_gain

    g_bc = jnp.stack([part[2] for part in large])
    bc_got = swap(lax.dynamic_slice_in_dim(g_bc, (1 - mine) * bc_rows, bc_rows, 1))
    g_bc = lax.dynamic_slice_in_dim(g_bc, mine * bc_rows, bc_rows, 1) + bc_got
    hidden = hidden + (last_own + after(last_got, settled).astype(f32))
    shared = jnp.concatenate([e[0] for e in early] + late, axis=0)
    shared = shared + swap(shared)
    small = butterfly(jnp.concatenate([shared] + [part for e in early for part in e[1:]], axis=0))
    at = 0

    def take(*shape):
        nonlocal at
        size = 1
        for s in shape:
            size *= s
        at += size // LANES
        return small[at - size // LANES : at].reshape(shape)

    r_state = jnp.stack([take(5, 2 * LANES) for _ in range(layers)])
    r_gain = jnp.stack([take(width) for _ in range(layers)])
    r_inner, r_head = zip(*[(take(7, inner), take(2, LANES)) for _ in range(layers)])
    r_inner, r_head = jnp.stack(r_inner), jnp.stack(r_head)[:, :, :heads]
    g_z, g_x, _, g_dt, g_out = (jnp.stack(parts) for parts in zip(*large))
    return (
        hidden, flow, r_gain, g_z, g_x, g_bc, g_dt,
        r_inner[:, :4], r_inner[:, 4], r_state[:, :4], r_state[:, 4],
        r_head[:, 0], r_head[:, 1],
        jnp.sum(r_inner[:, 5].reshape(layers, heads, HEADDIM), axis=2), r_inner[:, 6], g_out,
    )


def solution(mesh):
    row = P(("dp", "tensor"), None)
    rest = (
        P(), P(None, "dp", "tensor"), P(None, "dp", "tensor"), P(None, ("dp", "tensor"), None),
        P(None, "dp", "tensor"), P(None, None, "tensor"), P(None, "tensor"), P(), P(),
        P(None, "tensor"), P(None, "tensor"), P(None, "tensor"), P(None, "tensor"),
        P(None, "tensor", "dp"),
    )
    specs = (row, row, *rest)
    return jax.shard_map(local, mesh=mesh, in_specs=specs, out_specs=specs, check_vma=False)
```
